512 devices in a mesh: dp: 16 (over z, core), ent: 32 (over y, x).
Axes of the slice: x: 4, y: 8, z: 8, core: 2. Of those that a mesh axis runs over, the one named last changes fastest.
Arguments:
- entity_table: float32 [16384, 1024], P('ent')
- adagrad_state: float32 [16384], P('ent'), may hold values from 0.0001 to 0.01
- relation_phase: float32 [448, 512], replicated, may hold values from -3.140625 to 3.140625
- head_owner: int32 [65536, 1], P(('dp', 'ent')), may hold values from 0 to 31; in each aligned block of 128 rows (0 to 127, 128 to 255, ...) at most 12 rows name the same one
- head_row: int32 [65536], P(('dp', 'ent')), may hold values from 0 to 511
- relation_id: int32 [65536], P(('dp', 'ent')), may hold values from 0 to 447
- tail_row: int32 [65536], P(('dp', 'ent')), may hold values from 0 to 511
- negative_row: int32 [1048576], P(('dp', 'ent')), may hold values from 0 to 511
Outputs:
- new_table: float32 [16384, 1024], P('ent')
- new_state: float32 [16384], P('ent')
The draws below stay inside these ranges and needn't reach their ends.
Inputs may be any that keep to these rules, and one draw needn't show every extreme that they name: `head_owner`: within each aligned block of 128 triples (those of one device) no index is named more than 12 times, a bound that some block reaches.
All inputs are finite; a program needn't handle non-finite values.
Results may differ from the reference program's by a relative error of at most 0.0014.
Values may be sent and summed in bfloat16 or wider, within the bound.
A program may use at most 64 MiB of HBM per device.

```python
import math
import jax
import jax.numpy as jnp
import numpy as np
from jax import lax

K = 512
RELS = 448
ROWS_DEV = 512
TRI_DEV = 128
NEG_DEV = 2048
CAP = 12
ENTITIES = 16384
TRIPLES = 65536
NEGS = 1048576
N_DP = 16
N_ENT = 32


def draw_entity_table(key, part):
    key_scale, key_value = jax.random.split(jax.random.fold_in(key, 11))
    lowest, highest = (0.35, 3.5)
    values = jax.random.normal(key_value, (ENTITIES, 2 * K), jnp.float32)
    scales = jnp.exp(jax.random.uniform(key_scale, (ENTITIES, 1), jnp.float32, math.log(lowest), math.log(highest)))
    return values * scales


def with_ends(values, key, least, top_value):
    longest = values.shape.index(max(values.shape))
    spots = []
    for shift in (0, 1):
        where = [jax.random.randint(jax.random.fold_in(key, axis), (), 0, length) for axis, length in enumerate(values.shape)]
        where[longest] = (where[longest] + shift) % values.shape[longest]
        spots.append(tuple(where))
    return values.at[spots[0]].set(least).at[spots[1]].set(top_value)


def block_levels(own_key, extent, pieces, smallest, high):
    loudness = 1.0
    for dim, blocks in pieces:
        steps = jax.random.uniform(jax.random.fold_in(jax.random.fold_in(own_key, 6), dim), (blocks,), jnp.float32, smallest / len(pieces), high / len(pieces))
        loudness = loudness * jnp.repeat(jnp.exp(steps), extent[dim] // blocks).reshape((-1,) + (1,) * (len(extent) - 1 - dim))
    return loudness


def shared_out(rng, own, number, rows, count, top, reach, slope):
    order = jax.random.permutation(rng, count)
    crowded, common = load_shares(count, rows * top, reach, slope, True), load_shares(count, rows * top, reach, slope, False)
    places = jnp.arange(count)

    def named(tallies, turn):
        used = int((tallies > 0).sum())
        fixed = max(1, used // 4)
        moved = fixed + (places - fixed + turn * (used - fixed)) % max(1, count - fixed)
        return jnp.zeros((count,), jnp.int32).at[order[jnp.where(places < fixed, places, moved)]].set(jnp.asarray(tallies, jnp.int32))

    tallies = jnp.where(number % 4 == 0, named(crowded, number // 4), named(common, number - number // 4 - 1))
    mixed = jax.random.permutation(jax.random.fold_in(own, 3), count)
    giver, taker = mixed[0:count // 2 * 2:2], mixed[1:count // 2 * 2:2]
    slack = jnp.minimum(tallies[giver] - 1, reach - tallies[taker]) // 2
    slack = jnp.where((giver == order[0]) | (taker == order[0]) | (tallies[taker] == 0), 0, jnp.maximum(slack, 0))
    moved = jax.random.randint(jax.random.fold_in(own, 4), (count // 2,), 0, 1 << 20) % (slack + 1)
    tallies = tallies.at[giver].add(-moved).at[taker].add(moved)
    members = jnp.searchsorted(jnp.cumsum(tallies), jnp.arange(rows * top), side="right").astype(jnp.int32)
    listing = members.reshape(top, rows).T
    listing = listing[jax.random.permutation(jax.random.fold_in(own, 1), rows)]
    turn = jax.random.randint(jax.random.fold_in(own, 2), (rows, 1), 0, top)
    return jnp.take_along_axis(listing, (jnp.arange(top)[None, :] + turn) % top, axis=1)


def load_shares(number_of, total, reach, slope, full):
    loads = [(1 << 20) // math.isqrt(rank ** slope) + 1 for rank in range(1, number_of + 1)]
    largest = reach if full else min(reach, max(-(-total // number_of), total * loads[0] // sum(loads)))
    least = 1 if total - largest >= number_of - 1 else 0
    counts, surplus = [largest] + [least] * (number_of - 1), total - largest - least * (number_of - 1)
    while surplus > 0:
        movable = [i for i in range(1, number_of) if counts[i] < largest] or [i for i in range(1, number_of) if counts[i] < reach]
        pool, remaining = sum([loads[i] for i in movable]), surplus
        for i in movable:
            addition = min(reach - counts[i], max(1, remaining * loads[i] // pool), surplus)
            counts[i] = counts[i] + addition
            surplus = surplus - addition
    return np.array(counts)


def setup_inputs(seed: int = 0) -> dict:
    streams_of = jax.random.split(jax.random.key(seed), 9)
    entity_table = draw_entity_table(jax.random.fold_in(streams_of[8], 71), 0)
    adagrad_state = jnp.clip(jnp.exp(math.log(0.01) - 4.6051702 * jax.random.uniform(streams_of[1], (ENTITIES,), jnp.float32) ** block_levels(streams_of[1], (ENTITIES,), ((0, 32),), -0.2, 0.2)), 0.0001, 0.01)
    relation_phase = jnp.clip(jax.random.uniform(streams_of[2], (RELS, K), jnp.float32, -3.140625, 3.140625), -3.140625, 3.140625)
    head_owner_keys = jax.random.split(jax.random.fold_in(streams_of[3], 1), TRIPLES // TRI_DEV)
    head_owner_turns = jax.random.permutation(jax.random.fold_in(streams_of[3], 3), TRIPLES // TRI_DEV)
    head_owner = jax.vmap(lambda own, number: shared_out(jax.random.fold_in(streams_of[3], 2), own, number, TRI_DEV, N_ENT, 1, CAP, 2))(head_owner_keys, head_owner_turns).reshape((TRIPLES, 1))
    head_row = with_ends(jax.random.randint(streams_of[4], (TRIPLES,), 0, ROWS_DEV), jax.random.fold_in(streams_of[4], 1), 0, ROWS_DEV - 1).astype(jnp.int32)
    relation_id = with_ends(jax.random.randint(streams_of[5], (TRIPLES,), 0, RELS), jax.random.fold_in(streams_of[5], 1), 0, RELS - 1).astype(jnp.int32)
    tail_row = with_ends(jax.random.randint(streams_of[6], (TRIPLES,), 0, ROWS_DEV), jax.random.fold_in(streams_of[6], 1), 0, ROWS_DEV - 1).astype(jnp.int32)
    negative_row = with_ends(jax.random.randint(streams_of[7], (NEGS,), 0, ROWS_DEV), jax.random.fold_in(streams_of[7], 1), 0, ROWS_DEV - 1).astype(jnp.int32)
    return dict(entity_table=entity_table, adagrad_state=adagrad_state, relation_phase=relation_phase, head_owner=head_owner, head_row=head_row, relation_id=relation_id, tail_row=tail_row, negative_row=negative_row)


MARGIN = 12.0
LEARN_RATE = 0.25

def rotate(real_part, imag_part, cosine, sine_val):
    return (real_part * cosine - imag_part * sine_val, real_part * sine_val + imag_part * cosine)

def adagrad(rows_in, acc_in, gradient):
    new_acc = acc_in + lax.optimization_barrier(jnp.mean(gradient * gradient, axis=1))
    return (rows_in - LEARN_RATE * gradient / jnp.sqrt(new_acc)[:, None], new_acc)

def device_step(shard, shard_bf, head_bf, angles, tails, negatives):
    local_rows = shard.shape[0]
    half = shard.shape[1] // 2
    shard_wide = shard_bf.astype(jnp.float32)
    head_rows = head_bf.astype(jnp.float32)
    cosine = jnp.cos(angles)
    sine_val = jnp.sin(angles)
    rot_re, rot_im = rotate(head_rows[:, :half], head_rows[:, half:], cosine, sine_val)
    rotated = jnp.concatenate([rot_re, rot_im], axis=1)
    rotated_bf = rotated.astype(jnp.bfloat16)
    rotated_wide = rotated_bf.astype(jnp.float32)
    scores = jnp.dot(rotated_wide, shard_wide.T, precision=lax.Precision.HIGHEST)
    rot_sq = lax.optimization_barrier(jnp.sum(rotated * rotated, axis=1))
    row_sq = lax.optimization_barrier(jnp.sum(shard * shard, axis=1))
    distance = (rot_sq[:, None] + jnp.take(row_sq, negatives)[None, :] - 2.0 * jnp.take(scores, negatives, axis=1)) / half
    positive = jnp.take(shard, tails, axis=0)
    diff_pos = rotated - positive
    dist_pos = lax.optimization_barrier(jnp.sum(diff_pos * diff_pos, axis=1)) / half
    logits = MARGIN - distance
    shifted = jnp.exp(logits - lax.optimization_barrier(jnp.max(logits, axis=1, keepdims=True)))
    weights = shifted / lax.optimization_barrier(jnp.sum(shifted, axis=1, keepdims=True))
    neg_coef = -0.5 * weights * jax.nn.sigmoid(MARGIN - distance)
    pos_coef = 0.5 * jax.nn.sigmoid(dist_pos - MARGIN)
    row_coef = jax.ops.segment_sum(neg_coef.T, negatives, num_segments=local_rows).T
    row_coef_bf = row_coef.astype(jnp.bfloat16)
    coef_wide = row_coef_bf.astype(jnp.float32)
    total_coef = pos_coef + lax.optimization_barrier(jnp.sum(row_coef, axis=1))
    pulled = jnp.dot(coef_wide, shard_wide, precision=lax.Precision.HIGHEST)
    grad_query = 2.0 / half * (total_coef[:, None] * rotated - pos_coef[:, None] * positive - pulled)
    grad_re, grad_im = rotate(grad_query[:, :half], grad_query[:, half:], cosine, -sine_val)
    grad_head = jnp.concatenate([grad_re, grad_im], axis=1)
    tail_pull = jnp.dot(coef_wide.T, rotated_wide, precision=lax.Precision.HIGHEST)
    column_coef = lax.optimization_barrier(jnp.sum(row_coef, axis=0))
    tail_part = 2.0 / half * (column_coef[:, None] * shard - tail_pull)
    tail_part = tail_part + jax.ops.segment_sum(-2.0 / half * pos_coef[:, None] * diff_pos, tails, num_segments=local_rows)
    return (grad_head, tail_part)

def reference(entity_table, adagrad_state, relation_phase, head_owner, head_row, relation_id, tail_row, negative_row):
    table_bf = entity_table.astype(jnp.bfloat16)
    shards = entity_table.reshape(N_ENT, ROWS_DEV, 2 * K)
    shards_bf = table_bf.reshape(N_ENT, ROWS_DEV, 2 * K)
    head_global = (head_owner[:, 0] * ROWS_DEV + head_row).astype(jnp.int32).reshape(N_DP, N_ENT, TRI_DEV)
    relations = relation_id.reshape(N_DP, N_ENT, TRI_DEV)
    tails = tail_row.reshape(N_DP, N_ENT, TRI_DEV)
    negatives = negative_row.reshape(N_DP, N_ENT, NEG_DEV)

    def group_step(total, inputs):
        heads_g, rel_g, tail_g, neg_g = inputs
        head_bf = jnp.take(table_bf, heads_g, axis=0)
        angles = jnp.take(relation_phase, rel_g, axis=0)
        grad_head, tail_part = jax.vmap(device_step)(shards, shards_bf, head_bf, angles, tail_g, neg_g)
        group_grad = tail_part.reshape(ENTITIES, 2 * K) + jax.ops.segment_sum(grad_head.reshape(N_ENT * TRI_DEV, 2 * K), heads_g.reshape(N_ENT * TRI_DEV), num_segments=ENTITIES)
        return (total + group_grad, None)
    total, _ = lax.scan(group_step, jnp.zeros((ENTITIES, 2 * K), jnp.float32), (head_global, relations, tails, negatives))
    new_table, new_state = adagrad(entity_table, adagrad_state, total)
    return (new_table, new_state)
```

```python
import functools

import jax
import jax.numpy as jnp
from jax import lax
from jax.experimental import pallas as pl
from jax.experimental.pallas import tpu as pltpu
from jax.sharding import PartitionSpec as P

MARGIN = 12.0
LEARN_RATE = 0.25
F32 = jnp.float32
BF16 = jnp.bfloat16
LANES = 128


def onehot(condition):
    return jnp.where(condition, 1.0, 0.0).astype(BF16)


def iota(shape, dim):
    return lax.broadcasted_iota(jnp.int32, shape, dim)


def to_column(row):
    wide = jnp.broadcast_to(row, (LANES, row.shape[1]))
    return jnp.transpose(wide)[:, 0:1]


def to_row(column):
    wide = jnp.broadcast_to(column, (column.shape[0], LANES))
    return jnp.transpose(wide)[0:1, :]


def dot(a, b):
    return jnp.dot(a, b, preferred_element_type=F32)


def dot_nt(a, b, precision=None):
    return lax.dot_general(
        a, b, (((1,), (1,)), ((), ())), preferred_element_type=F32, precision=precision
    )


def split3(x):
    first = x.astype(BF16)
    rest = x - first.astype(F32)
    second = rest.astype(BF16)
    third = (rest - second.astype(F32)).astype(BF16)
    return first, second, third


def kernel(
    n_ent,
    n_dp,
    cap,
    table_hbm,
    state_ref,
    phase_hbm,
    owner_ref,
    hrow_ref,
    rel_ref,
    tail_ref,
    neg_ref,
    out_table,
    out_state,
    table,
    table_bf,
    phase,
    flat,
    req_send,
    req_recv,
    rep_send,
    rep_recv,
    gr_send,
    gr_recv,
    pick,
    pick_t,
    asked,
    asked_t,
    tail_hot,
    row_sq,
    count,
    positive,
    cosine,
    sine,
    rotated,
    partial,
    pair_send,
    pair_recv,
    z_send,
    z_recv,
    total,
    state_col,
    sems,
):
    rows, width = table.shape
    half = width // 2
    tri = hrow_ref.shape[1]
    negs = neg_ref.shape[1]
    rels = phase.shape[0]
    slots = n_ent * cap
    chunks = width // LANES
    blk = cap * chunks
    nz = n_dp // 2
    hrows = rows // 2
    prow = rows // n_dp
    ny = n_ent // 4 if n_ent > 4 else 2
    nx = n_ent // ny
    tile = 256
    tiles = width // tile

    ent = lax.axis_index("ent")
    dp = lax.axis_index("dp")
    z = lax.div(dp, 2)
    core = lax.rem(dp, 2)
    y = lax.div(ent, nx)
    x = lax.rem(ent, nx)
    partner = dp + 1 - 2 * core

    def turn(m, n):
        odd = lax.rem(m, 2)
        return lax.rem((2 * odd - 1) * lax.div(m + 1, 2) + n, n)

    def ent_peer(k):
        dy = turn(lax.rem(k, ny), ny)
        dx = lax.div(k, ny)
        return lax.rem(y + dy, ny) * nx + lax.rem(x + dx, nx)

    def z_peer(k):
        return lax.rem(z + turn(nz - k, nz), nz)

    def remote(src, dst, first_sem, axis, index):
        return pltpu.make_async_remote_copy(
            src_ref=src,
            dst_ref=dst,
            send_sem=sems.at[first_sem],
            recv_sem=sems.at[first_sem + 1],
            device_id={axis: index},
            device_id_type=pl.DeviceIdType.MESH,
        )

    load_table = pltpu.make_async_copy(table_hbm, table, sems.at[0])
    load_phase = pltpu.make_async_copy(phase_hbm, phase, sems.at[1])
    load_table.start()
    load_phase.start()

    barrier = pltpu.get_barrier_semaphore()

    def greet_ent(k, carry):
        pl.semaphore_signal(
            barrier, inc=1, device_id={"ent": ent_peer(k)}, device_id_type=pl.DeviceIdType.MESH
        )
        return carry

    def greet_z(k, carry):
        pl.semaphore_signal(
            barrier,
            inc=1,
            device_id={"dp": 2 * z_peer(k) + core},
            device_id_type=pl.DeviceIdType.MESH,
        )
        return carry

    lax.fori_loop(1, n_ent, greet_ent, 0)
    lax.fori_loop(1, nz, greet_z, 0)
    pl.semaphore_signal(
        barrier, inc=1, device_id={"dp": partner}, device_id_type=pl.DeviceIdType.MESH
    )

    owner_row = owner_ref[...]
    own_hot = owner_row == iota((n_ent, tri), 0)
    own_bf = onehot(own_hot)
    before = onehot(iota((tri, tri), 0) < iota((tri, tri), 1))
    prior = dot(own_bf, before)
    rank = jnp.sum(jnp.where(own_hot, prior, 0.0), axis=0, keepdims=True).astype(jnp.int32)
    slot_row = owner_row * cap + rank
    lane_row = lax.rem(ent * cap + rank, LANES)
    lane_hot = onehot(lane_row == iota((LANES, tri), 0))
    wanted = hrow_ref[...] + 1
    high = lax.shift_right_logical(wanted, 5)
    low = wanted - high * 32
    high_part = jnp.where(own_hot, high.astype(F32), 0.0).astype(BF16)
    low_part = jnp.where(own_hot, low.astype(F32), 0.0).astype(BF16)
    request = dot_nt(high_part, lane_hot) * 32.0 + dot_nt(low_part, lane_hot)
    for o in range(n_ent):
        req_send[o] = request[o : o + 1, :]

    pl.semaphore_wait(barrier, n_ent - 1 + nz - 1 + 1)

    def send_request(k, carry):
        q = ent_peer(k)
        remote(req_send.at[q], req_recv.at[ent], 2, "ent", q).start()
        return carry

    lax.fori_loop(1, n_ent, send_request, 0)
    req_recv[ent] = req_send[ent]

    load_table.wait()

    def cast_table(j, carry):
        columns = pl.ds(pl.multiple_of(j * tile, tile), tile)
        table_bf[:, columns] = table[:, columns].astype(BF16)
        return carry

    lax.fori_loop(0, tiles, cast_table, 0)

    got = remote(
        req_send.at[pl.ds(0, n_ent - 1)], req_recv.at[pl.ds(0, n_ent - 1)], 2, "ent", ent_peer(1)
    )
    got.wait_recv()
    got.wait_send()

    inbox = jnp.concatenate([req_recv[o] for o in range(n_ent)], axis=0)
    first = iota((n_ent, LANES), 0) * cap
    lane = iota((n_ent, LANES), 1)
    offset = lax.rem(lane - first + LANES * n_ent, LANES)
    vreg = lax.shift_right_logical(first + offset, 7)
    ask_parts = []
    for v in range(-(-slots // LANES)):
        mine = jnp.logical_and(offset < cap, vreg == v)
        ask_parts.append(jnp.sum(jnp.where(mine, inbox, 0.0), axis=0, keepdims=True))
    ask_row = jnp.concatenate(ask_parts, axis=1)[:, :slots].astype(jnp.int32) - 1
    ask_col = to_column(ask_row)
    asked_t[...] = onehot(ask_col == iota((slots, rows), 1))

    def fetch(j, carry):
        columns = pl.ds(pl.multiple_of(j * tile, tile), tile)
        part = dot(asked_t[...], table_bf[:, columns])
        flat[pl.ds(2 * j, slots, stride=chunks), :] = part[:, :LANES]
        flat[pl.ds(2 * j + 1, slots, stride=chunks), :] = part[:, LANES:]
        return carry

    lax.fori_loop(0, tiles, fetch, 0)

    def send_rows(source, target, first_sem):
        def body(k, carry):
            q = ent_peer(k)
            block = pl.ds(pl.multiple_of(q * blk, 16), blk)
            source[block, :] = flat[block, :].astype(BF16)
            remote(
                source.at[block],
                target.at[pl.ds(pl.multiple_of(ent * blk, 16), blk)],
                first_sem,
                "ent",
                q,
            ).start()
            return carry

        lax.fori_loop(1, n_ent, body, 0)
        own = pl.ds(pl.multiple_of(ent * blk, 16), blk)
        target[own, :] = flat[own, :].astype(BF16)

    def wait_rows(source, target, first_sem):
        most = pl.ds(0, (n_ent - 1) * blk)
        done = remote(source.at[most], target.at[most], first_sem, "ent", ent_peer(1))
        done.wait_recv()
        done.wait_send()

    def unpack(target):
        def body(k, carry):
            block = pl.ds(pl.multiple_of(k * blk, 16), blk)
            flat[block, :] = target[block, :].astype(F32)
            return carry

        lax.fori_loop(0, n_ent, body, 0)

    def slot_tile(j):
        return jnp.concatenate(
            [
                flat[pl.ds(2 * j, slots, stride=chunks), :],
                flat[pl.ds(2 * j + 1, slots, stride=chunks), :],
            ],
            axis=1,
        ).astype(BF16)

    send_rows(rep_send, rep_recv, 4)

    asked[...] = onehot(ask_row == iota((rows, slots), 0))
    pick_t[...] = onehot(slot_row == iota((slots, tri), 0))
    pick[...] = onehot(to_column(slot_row) == iota((tri, slots), 1))

    neg = neg_ref[...]
    neg_high = lax.shift_right_logical(neg, 7)
    neg_low = neg - neg_high * LANES
    counts = dot_nt(
        onehot(neg_high == iota((8, negs), 0)), onehot(neg_low == iota((LANES, negs), 0))
    )
    count[...] = jnp.concatenate([counts[v : v + 1, :] for v in range(rows // LANES)], axis=1)

    tail_row = tail_ref[...]
    tail_hot[...] = onehot(tail_row == iota((rows, tri), 0))
    tail_pick = onehot(to_column(tail_row) == iota((tri, rows), 1))

    def tails(j, square):
        columns = pl.ds(pl.multiple_of(j * tile, tile), tile)
        part = table[:, columns]
        parts = split3(part)
        positive[:, columns] = (
            dot(tail_pick, parts[2]) + dot(tail_pick, parts[1]) + dot(tail_pick, parts[0])
        )
        return square + jnp.sum(part * part, axis=1, keepdims=True)

    row_sq[...] = to_row(lax.fori_loop(0, tiles, tails, jnp.zeros((rows, 1), F32)))

    load_phase.wait()
    rel_pick = onehot(to_column(rel_ref[...]) == iota((tri, rels), 1))

    def angles(j, carry):
        columns = pl.ds(pl.multiple_of(j * LANES, LANES), LANES)
        parts = split3(phase[:, columns])
        angle = dot(rel_pick, parts[2]) + dot(rel_pick, parts[1]) + dot(rel_pick, parts[0])
        cosine[:, columns] = jnp.cos(angle)
        sine[:, columns] = jnp.sin(angle)
        return carry

    lax.fori_loop(0, half // LANES, angles, 0)
    state_col[...] = to_column(state_ref[...])

    wait_rows(rep_send, rep_recv, 4)
    unpack(rep_recv)

    def rotate(j, sums):
        sums_rot, sums_diff = sums
        re = pl.ds(pl.multiple_of(j * tile, tile), tile)
        im = pl.ds(pl.multiple_of(half + j * tile, tile), tile)
        head_re = dot(pick[...], slot_tile(j))
        head_im = dot(pick[...], slot_tile(j + tiles // 2))
        cos, sin = cosine[:, re], sine[:, re]
        rot_re = head_re * cos - head_im * sin
        rot_im = head_re * sin + head_im * cos
        rotated[:, re] = rot_re
        rotated[:, im] = rot_im
        diff_re = rot_re - positive[:, re]
        diff_im = rot_im - positive[:, im]
        sums_rot += jnp.sum(rot_re * rot_re + rot_im * rot_im, axis=1, keepdims=True)
        sums_diff += jnp.sum(diff_re * diff_re + diff_im * diff_im, axis=1, keepdims=True)
        return sums_rot, sums_diff

    nothing = jnp.zeros((tri, 1), F32)
    rot_sq, diff_sq = lax.fori_loop(0, tiles // 2, rotate, (nothing, nothing))
    rotated_bf = rotated[...].astype(BF16)
    scores = dot_nt(rotated_bf, table_bf[...])
    distance = (rot_sq + row_sq[...] - 2.0 * scores) * (1.0 / half)
    dist_pos = diff_sq * (1.0 / half)
    logits = MARGIN - distance
    times = count[...]
    named = times > 0.0
    masked = jnp.where(named, logits, -jnp.inf)
    shifted = times * jnp.exp(masked - jnp.max(masked, axis=1, keepdims=True))
    weights = shifted / jnp.sum(shifted, axis=1, keepdims=True)
    row_coef = -0.5 * weights * jax.nn.sigmoid(logits)
    pos_coef = 0.5 * jax.nn.sigmoid(dist_pos - MARGIN)
    row_coef_bf = row_coef.astype(BF16)
    total_coef = pos_coef + jnp.sum(row_coef, axis=1, keepdims=True)

    def head_grad(j, carry):
        re = pl.ds(pl.multiple_of(j * tile, tile), tile)
        im = pl.ds(pl.multiple_of(half + j * tile, tile), tile)
        out = []
        for columns in (re, im):
            pulled = dot(row_coef_bf, table_bf[:, columns])
            out.append(
                2.0
                / half
                * (total_coef * rotated[:, columns] - pos_coef * positive[:, columns] - pulled)
            )
        cos, sin = cosine[:, re], sine[:, re]
        grad_re = (out[0] * cos + out[1] * sin).astype(BF16)
        grad_im = (out[1] * cos - out[0] * sin).astype(BF16)
        for at, value in ((j, grad_re), (j + tiles // 2, grad_im)):
            part = dot(pick_t[...], value)
            flat[pl.ds(2 * at, slots, stride=chunks), :] = part[:, :LANES]
            flat[pl.ds(2 * at + 1, slots, stride=chunks), :] = part[:, LANES:]
        return carry

    lax.fori_loop(0, tiles // 2, head_grad, 0)
    send_rows(gr_send, gr_recv, 6)

    scale = 2.0 / half
    turned = jnp.transpose(row_coef)
    column = jnp.sum(turned, axis=1, keepdims=True) * scale
    turned_bf = turned.astype(BF16)
    pos_scaled = pos_coef * -scale

    def own_part(j, carry):
        columns = pl.ds(pl.multiple_of(j * tile, tile), tile)
        rot = rotated[:, columns]
        push = pos_scaled * (rot - positive[:, columns])
        push_high = push.astype(BF16)
        push_low = (push - push_high.astype(F32)).astype(BF16)
        partial[:, columns] = (
            column * table[:, columns]
            - scale * dot(turned_bf, rot.astype(BF16))
            + dot(tail_hot[...], push_high)
            + dot(tail_hot[...], push_low)
        )
        return carry

    lax.fori_loop(0, tiles, own_part, 0)

    wait_rows(gr_send, gr_recv, 6)
    unpack(gr_recv)

    theirs = pl.ds(pl.multiple_of((1 - core) * hrows, hrows), hrows)
    ours = pl.ds(pl.multiple_of(core * hrows, hrows), hrows)

    def add_theirs(j, carry):
        columns = pl.ds(pl.multiple_of(j * tile, tile), tile)
        pair_send[:, columns] = (
            partial[theirs, columns] + dot(asked[theirs, :], slot_tile(j))
        ).astype(BF16)
        return carry

    lax.fori_loop(0, tiles, add_theirs, 0)
    pair = remote(pair_send, pair_recv, 8, "dp", partner)
    pair.start()

    def add_ours(j, carry):
        columns = pl.ds(pl.multiple_of(j * tile, tile), tile)
        partial[ours, columns] += dot(asked[ours, :], slot_tile(j))
        return carry

    lax.fori_loop(0, tiles, add_ours, 0)
    pair.wait_recv()

    def piece_of(index):
        block = pl.ds(pl.multiple_of(index * prow, prow), prow)
        mine = pl.ds(pl.multiple_of(core * hrows + index * prow, prow), prow)
        return (partial[mine, :] + pair_recv[block, :].astype(F32)).astype(BF16)

    def send_piece(k, carry):
        to = z_peer(k)
        z_send[to] = piece_of(to)
        remote(z_send.at[to], z_recv.at[z], 10, "dp", 2 * to + core).start()
        return carry

    lax.fori_loop(1, nz, send_piece, 0)
    z_recv[z] = piece_of(z)
    pieces = remote(z_send.at[pl.ds(0, nz - 1)], z_recv.at[pl.ds(0, nz - 1)], 10, "dp", partner)
    pieces.wait_recv()

    def add_piece(k, value):
        return value + z_recv[k].astype(F32)

    here = pl.ds(pl.multiple_of(core * hrows + z * prow, prow), prow)
    total[here, :] = lax.fori_loop(1, nz, add_piece, z_recv[0].astype(F32)).astype(BF16)

    def send_total(k, carry):
        remote(total.at[here], total.at[here], 12, "dp", 2 * z_peer(k) + core).start()
        return carry

    lax.fori_loop(1, nz, send_total, 0)
    most = pl.ds(0, (nz - 1) * prow)
    spread = remote(total.at[most], total.at[most], 12, "dp", partner)
    spread.wait_recv()
    swap = remote(total.at[ours], total.at[ours], 14, "dp", partner)
    swap.start()

    def update(first_row):
        def body(k, carry):
            block = pl.ds(pl.multiple_of(first_row + k * 32, 32), 32)
            value = total[block, :].astype(F32)
            new = state_col[block, :] + jnp.sum(value * value, axis=1, keepdims=True) / width
            state_col[block, :] = new
            out_table[block, :] = table[block, :] - value * (LEARN_RATE / jnp.sqrt(new))
            return carry

        lax.fori_loop(0, hrows // 32, body, 0)

    update(core * hrows)
    swap.wait_recv()
    update((1 - core) * hrows)
    out_state[...] = to_row(state_col[...])
    pair.wait_send()
    pieces.wait_send()
    spread.wait_send()
    swap.wait_send()


def on_device(
    n_ent,
    n_dp,
    entity_table,
    adagrad_state,
    relation_phase,
    head_owner,
    head_row,
    relation_id,
    tail_row,
    negative_row,
):
    rows, width = entity_table.shape
    rels, half = relation_phase.shape
    tri = head_row.shape[0]
    negs = negative_row.shape[0]
    cap = 12
    slots = n_ent * cap
    chunks = width // LANES
    hrows = rows // 2
    prow = rows // n_dp
    nz = n_dp // 2
    vmem = pl.BlockSpec(memory_space=pltpu.VMEM)
    anywhere = pl.BlockSpec(memory_space=pl.ANY)
    new_table, new_state = pl.pallas_call(
        functools.partial(kernel, n_ent, n_dp, cap),
        out_shape=(
            jax.ShapeDtypeStruct((rows, width), F32),
            jax.ShapeDtypeStruct((1, rows), F32),
        ),
        in_specs=[anywhere, vmem, anywhere, vmem, vmem, vmem, vmem, vmem],
        out_specs=(vmem, vmem),
        scratch_shapes=[
            pltpu.VMEM((rows, width), F32),
            pltpu.VMEM((rows, width), BF16),
            pltpu.VMEM((rels, half), F32),
            pltpu.VMEM((slots * chunks, LANES), F32),
            pltpu.VMEM((n_ent, 1, LANES), F32),
            pltpu.VMEM((n_ent, 1, LANES), F32),
            pltpu.VMEM((slots * chunks, LANES), BF16),
            pltpu.VMEM((slots * chunks, LANES), BF16),
            pltpu.VMEM((slots * chunks, LANES), BF16),
            pltpu.VMEM((slots * chunks, LANES), BF16),
            pltpu.VMEM((tri, slots), BF16),
            pltpu.VMEM((slots, tri), BF16),
            pltpu.VMEM((rows, slots), BF16),
            pltpu.VMEM((slots, rows), BF16),
            pltpu.VMEM((rows, tri), BF16),
            pltpu.VMEM((1, rows), F32),
            pltpu.VMEM((1, rows), F32),
            pltpu.VMEM((tri, width), F32),
            pltpu.VMEM((tri, half), F32),
            pltpu.VMEM((tri, half), F32),
            pltpu.VMEM((tri, width), F32),
            pltpu.VMEM((rows, width), F32),
            pltpu.VMEM((hrows, width), BF16),
            pltpu.VMEM((hrows, width), BF16),
            pltpu.VMEM((nz, prow, width), BF16),
            pltpu.VMEM((nz, prow, width), BF16),
            pltpu.VMEM((rows, width), BF16),
            pltpu.VMEM((rows, 1), F32),
            pltpu.SemaphoreType.DMA((16,)),
        ],
        compiler_params=pltpu.CompilerParams(
            collective_id=0, has_side_effects=True, vmem_limit_bytes=48 * 1024 * 1024
        ),
    )(
        entity_table,
        adagrad_state.reshape(1, rows),
        relation_phase,
        head_owner.reshape(1, tri),
        head_row.reshape(1, tri),
        relation_id.reshape(1, tri),
        tail_row.reshape(1, tri),
        negative_row.reshape(1, negs),
    )
    return new_table, new_state.reshape(rows)


def solution(mesh):
    return jax.shard_map(
        functools.partial(on_device, mesh.shape["ent"], mesh.shape["dp"]),
        mesh=mesh,
        in_specs=(
            P("ent", None),
            P("ent"),
            P(),
            P(("dp", "ent"), None),
            P(("dp", "ent")),
            P(("dp", "ent")),
            P(("dp", "ent")),
            P(("dp", "ent")),
        ),
        out_specs=(P("ent", None), P("ent")),
        check_vma=False,
    )
```

```python
import functools

import jax
import jax.numpy as jnp
from jax import lax
from jax.experimental import pallas as pl
from jax.experimental.pallas import tpu as pltpu
from jax.sharding import PartitionSpec as P

MARGIN = 12.0
LEARN_RATE = 0.25
F32 = jnp.float32
BF16 = jnp.bfloat16
LANES = 128


def onehot(condition):
    return jnp.where(condition, 1.0, 0.0).astype(BF16)


def iota(shape, dim):
    return lax.broadcasted_iota(jnp.int32, shape, dim)


def to_column(row):
    wide = jnp.broadcast_to(row, (LANES, row.shape[1]))
    return jnp.transpose(wide)[:, 0:1]


def to_row(column):
    wide = jnp.broadcast_to(column, (column.shape[0], LANES))
    return jnp.transpose(wide)[0:1, :]


def dot(a, b):
    return jnp.dot(a, b, preferred_element_type=F32)


def dot_nt(a, b, precision=None):
    return lax.dot_general(
        a, b, (((1,), (1,)), ((), ())), preferred_element_type=F32, precision=precision
    )


def split3(x):
    first = x.astype(BF16)
    rest = x - first.astype(F32)
    second = rest.astype(BF16)
    third = (rest - second.astype(F32)).astype(BF16)
    return first, second, third


def kernel(
    n_ent,
    n_dp,
    cap,
    table_hbm,
    state_hbm,
    phase_hbm,
    owner_hbm,
    hrow_hbm,
    rel_hbm,
    tail_hbm,
    neg_hbm,
    out_table,
    out_state,
    table,
    table_bf,
    phase,
    state_ref,
    owner_ref,
    hrow_ref,
    rel_ref,
    tail_ref,
    neg_ref,
    flat,
    req_send,
    req_recv,
    rep_send,
    rep_recv,
    gr_send,
    gr_recv,
    pick,
    pick_t,
    asked,
    asked_t,
    tail_hot,
    row_sq,
    count,
    positive,
    cosine,
    sine,
    rotated,
    partial,
    pair_send,
    pair_recv,
    ring_send,
    ring_recv,
    total,
    state_col,
    gr_flat_0,
    gr_flat_1,
    sems,
    load_sems,
    ring_sems,
    spread_sems,
):
    rows, width = table.shape
    half = width // 2
    gr_flat = (gr_flat_0, gr_flat_1)
    tri = hrow_ref.shape[1]
    negs = neg_ref.shape[1]
    rels = phase.shape[0]
    slots = n_ent * cap
    chunks = width // LANES
    blk = cap * chunks
    nz = n_dp // 2
    hrows = rows // 2
    prow = rows // n_dp
    ny = n_ent // 4 if n_ent > 4 else 2
    nx = n_ent // ny
    tile = 256
    tiles = width // tile

    ent = lax.axis_index("ent")
    dp = lax.axis_index("dp")
    z = lax.div(dp, 2)
    core = lax.rem(dp, 2)
    y = lax.div(ent, nx)
    x = lax.rem(ent, nx)
    partner = dp + 1 - 2 * core

    def shift(m, n):
        return ((m + 1) // 2 if m % 2 else -(m // 2)) % n

    def ent_peer(k):
        return lax.rem(y + shift(k % ny, ny), ny) * nx + lax.rem(x + k // ny, nx)

    def z_peer(k):
        return lax.rem(z + shift(nz - k, nz), nz)

    def remote(src, dst, send_sem, recv_sem, axis, index):
        return pltpu.make_async_remote_copy(
            src_ref=src,
            dst_ref=dst,
            send_sem=send_sem,
            recv_sem=recv_sem,
            device_id={axis: index},
            device_id_type=pl.DeviceIdType.MESH,
        )

    loads = [
        pltpu.make_async_copy(source, target, load_sems.at[i])
        for i, (source, target) in enumerate(
            (
                (owner_hbm, owner_ref),
                (hrow_hbm, hrow_ref),
                (table_hbm, table),
                (tail_hbm, tail_ref),
                (rel_hbm, rel_ref),
                (neg_hbm, neg_ref),
                (state_hbm, state_ref),
                (phase_hbm, phase),
            )
        )
    ]
    for load in loads:
        load.start()

    barrier = pltpu.get_barrier_semaphore()

    def greet(axis, index):
        pl.semaphore_signal(
            barrier, inc=1, device_id={axis: index}, device_id_type=pl.DeviceIdType.MESH
        )

    for k in range(1, n_ent):
        greet("ent", ent_peer(k))
    for k in range(1, nz):
        greet("dp", 2 * z_peer(k) + core)
    greet("dp", partner)

    loads[0].wait()
    loads[1].wait()
    owner_row = owner_ref[...]
    own_hot = owner_row == iota((n_ent, tri), 0)
    own_bf = onehot(own_hot)
    before = onehot(iota((tri, tri), 0) < iota((tri, tri), 1))
    prior = dot(own_bf, before)
    rank = jnp.sum(jnp.where(own_hot, prior, 0.0), axis=0, keepdims=True).astype(jnp.int32)
    slot_row = owner_row * cap + rank
    lane_row = lax.rem(ent * cap + rank, LANES)
    lane_hot = onehot(lane_row == iota((LANES, tri), 0))
    wanted = hrow_ref[...] + 1
    high = lax.shift_right_logical(wanted, 5)
    low = wanted - high * 32
    high_part = jnp.where(own_hot, high.astype(F32), 0.0).astype(BF16)
    low_part = jnp.where(own_hot, low.astype(F32), 0.0).astype(BF16)
    request = dot_nt(high_part, lane_hot) * 32.0 + dot_nt(low_part, lane_hot)
    for o in range(n_ent):
        req_send[o] = request[o : o + 1, :]

    pl.semaphore_wait(barrier, n_ent - 1 + nz - 1 + 1)

    for k in range(1, n_ent):
        q = ent_peer(k)
        remote(req_send.at[q], req_recv.at[ent], sems.at[0], sems.at[1], "ent", q).start()
    req_recv[ent] = req_send[ent]

    loads[2].wait()

    def cast_table(j, carry):
        columns = pl.ds(pl.multiple_of(j * tile, tile), tile)
        table_bf[:, columns] = table[:, columns].astype(BF16)
        return carry

    lax.fori_loop(0, tiles, cast_table, 0)

    most = pl.ds(0, n_ent - 1)
    got = remote(
        req_send.at[most], req_recv.at[most], sems.at[0], sems.at[1], "ent", ent_peer(1)
    )
    got.wait_recv()
    got.wait_send()

    inbox = jnp.concatenate([req_recv[o] for o in range(n_ent)], axis=0)
    first = iota((n_ent, LANES), 0) * cap
    lane = iota((n_ent, LANES), 1)
    offset = lax.rem(lane - first + LANES * n_ent, LANES)
    vreg = lax.shift_right_logical(first + offset, 7)
    ask_parts = []
    for v in range(-(-slots // LANES)):
        mine = jnp.logical_and(offset < cap, vreg == v)
        ask_parts.append(jnp.sum(jnp.where(mine, inbox, 0.0), axis=0, keepdims=True))
    ask_row = jnp.concatenate(ask_parts, axis=1)[:, :slots].astype(jnp.int32) - 1
    ask_col = to_column(ask_row)
    asked_t[...] = onehot(ask_col == iota((slots, rows), 1))

    def fetch(j, carry):
        columns = pl.ds(pl.multiple_of(j * tile, tile), tile)
        part = dot(asked_t[...], table_bf[:, columns])
        flat[pl.ds(2 * j, slots, stride=chunks), :] = part[:, :LANES]
        flat[pl.ds(2 * j + 1, slots, stride=chunks), :] = part[:, LANES:]
        return carry

    lax.fori_loop(0, tiles, fetch, 0)

    def send_rows(buffer, source, target, sem):
        size = buffer.shape[0] // n_ent
        own = pl.ds(pl.multiple_of(ent * size, 16), size)
        for k in range(1, n_ent):
            q = ent_peer(k)
            block = pl.ds(pl.multiple_of(q * size, 16), size)
            source[block, :] = buffer[block, :].astype(BF16)
            remote(
                source.at[block], target.at[own], sems.at[sem], sems.at[sem + 1], "ent", q
            ).start()
        target[own, :] = buffer[own, :].astype(BF16)

    def wait_rows(source, target, sem):
        most = pl.ds(0, target.shape[0] // n_ent * (n_ent - 1))
        done = remote(
            source.at[most], target.at[most], sems.at[sem], sems.at[sem + 1], "ent", ent_peer(1)
        )
        done.wait_recv()
        done.wait_send()

    def unpack(target, buffer):
        size = buffer.shape[0] // n_ent

        def body(k, carry):
            block = pl.ds(pl.multiple_of(k * size, 16), size)
            buffer[block, :] = target[block, :].astype(F32)
            return carry

        lax.fori_loop(0, n_ent, body, 0)

    def slot_tile(j):
        return jnp.concatenate(
            [
                flat[pl.ds(2 * j, slots, stride=chunks), :],
                flat[pl.ds(2 * j + 1, slots, stride=chunks), :],
            ],
            axis=1,
        ).astype(BF16)

    send_rows(flat, rep_send, rep_recv, 2)

    for load in loads[3:]:
        load.wait()
    asked[...] = onehot(ask_row == iota((rows, slots), 0))
    pick_t[...] = onehot(slot_row == iota((slots, tri), 0))
    pick[...] = onehot(to_column(slot_row) == iota((tri, slots), 1))

    neg = neg_ref[...]
    neg_high = lax.shift_right_logical(neg, 7)
    neg_low = neg - neg_high * LANES
    counts = dot_nt(
        onehot(neg_high == iota((8, negs), 0)), onehot(neg_low == iota((LANES, negs), 0))
    )
    count[...] = jnp.concatenate([counts[v : v + 1, :] for v in range(rows // LANES)], axis=1)

    tail_row = tail_ref[...]
    tail_hot[...] = onehot(tail_row == iota((rows, tri), 0))
    tail_pick = onehot(to_column(tail_row) == iota((tri, rows), 1))

    def tails(j, square):
        columns = pl.ds(pl.multiple_of(j * tile, tile), tile)
        part = table[:, columns]
        parts = split3(part)
        positive[:, columns] = (
            dot(tail_pick, parts[2]) + dot(tail_pick, parts[1]) + dot(tail_pick, parts[0])
        )
        return square + jnp.sum(part * part, axis=1, keepdims=True)

    row_sq[...] = to_row(lax.fori_loop(0, tiles, tails, jnp.zeros((rows, 1), F32)))

    rel_pick = onehot(to_column(rel_ref[...]) == iota((tri, rels), 1))

    def angles(j, carry):
        columns = pl.ds(pl.multiple_of(j * LANES, LANES), LANES)
        parts = split3(phase[:, columns])
        angle = dot(rel_pick, parts[2]) + dot(rel_pick, parts[1]) + dot(rel_pick, parts[0])
        cosine[:, columns] = jnp.cos(angle)
        sine[:, columns] = jnp.sin(angle)
        return carry

    lax.fori_loop(0, half // LANES, angles, 0)
    state_col[...] = to_column(state_ref[...])

    wait_rows(rep_send, rep_recv, 2)
    unpack(rep_recv, flat)

    def rotate(j, sums):
        sums_rot, sums_diff = sums
        re = pl.ds(pl.multiple_of(j * tile, tile), tile)
        im = pl.ds(pl.multiple_of(half + j * tile, tile), tile)
        head_re = dot(pick[...], slot_tile(j))
        head_im = dot(pick[...], slot_tile(j + tiles // 2))
        cos, sin = cosine[:, re], sine[:, re]
        rot_re = head_re * cos - head_im * sin
        rot_im = head_re * sin + head_im * cos
        rotated[:, re] = rot_re
        rotated[:, im] = rot_im
        diff_re = rot_re - positive[:, re]
        diff_im = rot_im - positive[:, im]
        sums_rot += jnp.sum(rot_re * rot_re + rot_im * rot_im, axis=1, keepdims=True)
        sums_diff += jnp.sum(diff_re * diff_re + diff_im * diff_im, axis=1, keepdims=True)
        return sums_rot, sums_diff

    nothing = jnp.zeros((tri, 1), F32)
    rot_sq, diff_sq = lax.fori_loop(0, tiles // 2, rotate, (nothing, nothing))
    rotated_bf = rotated[...].astype(BF16)
    scores = dot_nt(rotated_bf, table_bf[...])
    distance = (rot_sq + row_sq[...] - 2.0 * scores) * (1.0 / half)
    dist_pos = diff_sq * (1.0 / half)
    logits = MARGIN - distance
    times = count[...]
    named = times > 0.0
    masked = jnp.where(named, logits, -jnp.inf)
    shifted = times * jnp.exp(masked - jnp.max(masked, axis=1, keepdims=True))
    weights = shifted / jnp.sum(shifted, axis=1, keepdims=True)
    row_coef = -0.5 * weights * jax.nn.sigmoid(logits)
    pos_coef = 0.5 * jax.nn.sigmoid(dist_pos - MARGIN)
    row_coef_bf = row_coef.astype(BF16)
    total_coef = pos_coef + jnp.sum(row_coef, axis=1, keepdims=True)

    quarter = half // 2
    for h in range(2):
        re = pl.ds(h * quarter, quarter)
        im = pl.ds(half + h * quarter, quarter)
        out = []
        for columns in (re, im):
            pulled = dot(row_coef_bf, table_bf[:, columns])
            out.append(
                2.0
                / half
                * (total_coef * rotated[:, columns] - pos_coef * positive[:, columns] - pulled)
            )
        cos, sin = cosine[:, re], sine[:, re]
        grad_re = (out[0] * cos + out[1] * sin).astype(BF16)
        grad_im = (out[1] * cos - out[0] * sin).astype(BF16)
        for at, value in ((0, grad_re), (2, grad_im)):
            part = dot(pick_t[...], value)
            gr_flat[h][pl.ds(at, slots, stride=4), :] = part[:, :LANES]
            gr_flat[h][pl.ds(at + 1, slots, stride=4), :] = part[:, LANES:]
        send_rows(gr_flat[h], gr_send.at[h], gr_recv.at[h], 4 + 2 * h)

    scale = 2.0 / half
    turned = jnp.transpose(row_coef)
    column = jnp.sum(turned, axis=1, keepdims=True) * scale
    turned_bf = turned.astype(BF16)
    pos_scaled = pos_coef * -scale

    def own_part(h):
        def body(part, carry):
            columns = pl.ds(pl.multiple_of(part * half + h * quarter, quarter), quarter)
            rot = rotated[:, columns]
            push = pos_scaled * (rot - positive[:, columns])
            push_high = push.astype(BF16)
            push_low = (push - push_high.astype(F32)).astype(BF16)
            partial[h, :, pl.ds(pl.multiple_of(part * quarter, quarter), quarter)] = (
                column * table[:, columns]
                - scale * dot(turned_bf, rot.astype(BF16))
                + dot(tail_hot[...], push_high)
                + dot(tail_hot[...], push_low)
            )
            return carry

        lax.fori_loop(0, 2, body, 0)

    theirs = pl.ds(pl.multiple_of((1 - core) * hrows, hrows), hrows)
    ours = pl.ds(pl.multiple_of(core * hrows, hrows), hrows)
    longer, shorter = nz // 2, nz - 1 - nz // 2

    def rows_of(index):
        return pl.ds(pl.multiple_of(core * hrows + index * prow, prow), prow)

    def ways(h):
        lengths = (longer, shorter) if h == 0 else (shorter, longer)
        return [(w, (1, -1)[w], lengths[w]) for w in range(2) if lengths[w] > 0]

    def chip(distance):
        return lax.rem(z + distance + 2 * nz, nz)

    def add_incoming(h, some):
        def body(part, carry):
            columns = pl.ds(pl.multiple_of(part * quarter, quarter), quarter)
            value = jnp.concatenate(
                [
                    gr_flat[h][pl.ds(2 * part, slots, stride=4), :],
                    gr_flat[h][pl.ds(2 * part + 1, slots, stride=4), :],
                ],
                axis=1,
            ).astype(BF16)
            sums = partial[h, some, columns] + dot(asked[some, :], value)
            if some is theirs:
                pair_send[h, :, columns] = sums.astype(BF16)
            else:
                partial[h, some, columns] = sums
            return carry

        lax.fori_loop(0, 2, body, 0)

    def pair(h):
        return remote(
            pair_send.at[h], pair_recv.at[h], sems.at[8 + 2 * h], sems.at[9 + 2 * h], "dp", partner
        )

    def collect(h):
        wait_rows(gr_send.at[h], gr_recv.at[h], 4 + 2 * h)
        unpack(gr_recv.at[h], gr_flat[h])
        add_incoming(h, theirs)
        pair(h).start()
        add_incoming(h, ours)

    def take_pair(h):
        pair(h).wait_recv()
        partial[h, ours, :] += pair_recv[h].astype(F32)

    def ring(h, w, step, hop):
        return remote(
            ring_send.at[h, w, hop - 1],
            ring_recv.at[h, w, hop - 1],
            sems.at[12 + h],
            ring_sems.at[h, w, hop - 1],
            "dp",
            2 * chip(step) + core,
        )

    def sum_hop(h, hop):
        for w, step, length in ways(h):
            if hop <= length:
                value = partial[h, rows_of(chip(step * (length - hop + 1))), :]
                if hop > 1:
                    ring(h, w, step, hop - 1).wait_recv()
                    value += ring_recv[h, w, hop - 2].astype(F32)
                ring_send[h, w, hop - 1] = value.astype(BF16)
                ring(h, w, step, hop).start()

    def sum_end(h):
        value = partial[h, rows_of(z), :]
        for w, step, length in ways(h):
            ring(h, w, step, length).wait_recv()
            value += ring_recv[h, w, length - 1].astype(F32)
        total[h, rows_of(z), :] = value.astype(BF16)

    def spread(h, w, step, hop):
        piece = total.at[h, rows_of(chip(-step * (hop - 1)))]
        return remote(
            piece, piece, sems.at[14 + h], spread_sems.at[h, w, hop - 1], "dp", 2 * chip(step) + core
        )

    def across(h, piece):
        return remote(piece, piece, sems.at[16 + 2 * h], sems.at[17 + 2 * h], "dp", partner)

    def spread_hop(h, hop):
        if hop == 1:
            for w, step, length in ways(h):
                spread(h, w, step, 1).start()
            across(h, total.at[h, rows_of(z)]).start()
            return
        for w, step, length in ways(h):
            if hop <= length + 1:
                spread(h, w, step, hop - 1).wait_recv()
                if hop <= length:
                    spread(h, w, step, hop).start()
                across(h, total.at[h, rows_of(chip(-step * (hop - 1)))]).start()

    hops = longer
    own_part(0)
    own_part(1)
    collect(0)
    take_pair(0)
    for hop in range(1, hops + 1):
        sum_hop(0, hop)
    sum_end(0)
    spread_hop(0, 1)
    collect(1)
    take_pair(1)
    for hop in range(1, hops + 1):
        sum_hop(1, hop)
        spread_hop(0, hop + 1)
    sum_end(1)
    for hop in range(1, hops + 2):
        spread_hop(1, hop)

    def update(first_row):
        def body(k, carry):
            block = pl.ds(pl.multiple_of(first_row + k * 32, 32), 32)
            values = [total[h, block, :].astype(F32) for h in range(2)]
            square = values[0] * values[0] + values[1] * values[1]
            new = state_col[block, :] + jnp.sum(square, axis=1, keepdims=True) / width
            state_col[block, :] = new
            rate = LEARN_RATE / jnp.sqrt(new)
            for h in range(2):
                for part in range(2):
                    columns = pl.ds(part * half + h * quarter, quarter)
                    value = values[h][:, part * quarter : (part + 1) * quarter]
                    out_table[block, columns] = table[block, columns] - value * rate
            return carry

        lax.fori_loop(0, hrows // 32, body, 0)

    update(core * hrows)
    for h in range(2):
        across(h, total.at[h, theirs]).wait_recv()
    update((1 - core) * hrows)
    out_state[...] = to_row(state_col[...])
    for h in range(2):
        pair(h).wait_send()
        pieces = pl.ds(0, (nz - 1) * prow)
        piece = total.at[h, pieces]
        remote(piece, piece, sems.at[12 + h], sems.at[12 + h], "dp", partner).wait_send()
        remote(piece, piece, sems.at[14 + h], sems.at[14 + h], "dp", partner).wait_send()
        across(h, total.at[h, ours]).wait_send()


def on_device(
    n_ent,
    n_dp,
    entity_table,
    adagrad_state,
    relation_phase,
    head_owner,
    head_row,
    relation_id,
    tail_row,
    negative_row,
):
    rows, width = entity_table.shape
    rels, half = relation_phase.shape
    tri = head_row.shape[0]
    negs = negative_row.shape[0]
    cap = 12
    slots = n_ent * cap
    chunks = width // LANES
    hrows = rows // 2
    prow = rows // n_dp
    nz = n_dp // 2
    vmem = pl.BlockSpec(memory_space=pltpu.VMEM)
    hbm = pl.BlockSpec(memory_space=pltpu.HBM)
    new_table, new_state = pl.pallas_call(
        functools.partial(kernel, n_ent, n_dp, cap),
        out_shape=(
            jax.ShapeDtypeStruct((rows, width), F32),
            jax.ShapeDtypeStruct((1, rows), F32),
        ),
        in_specs=[hbm] * 8,
        out_specs=(vmem, vmem),
        scratch_shapes=[
            pltpu.VMEM((rows, width), F32),
            pltpu.VMEM((rows, width), BF16),
            pltpu.VMEM((rels, half), F32),
            pltpu.VMEM((1, rows), F32),
            pltpu.VMEM((1, tri), jnp.int32),
            pltpu.VMEM((1, tri), jnp.int32),
            pltpu.VMEM((1, tri), jnp.int32),
            pltpu.VMEM((1, tri), jnp.int32),
            pltpu.VMEM((1, negs), jnp.int32),
            pltpu.VMEM((slots * chunks, LANES), F32),
            pltpu.VMEM((n_ent, 1, LANES), F32),
            pltpu.VMEM((n_ent, 1, LANES), F32),
            pltpu.VMEM((slots * chunks, LANES), BF16),
            pltpu.VMEM((slots * chunks, LANES), BF16),
            pltpu.VMEM((2, slots * chunks // 2, LANES), BF16),
            pltpu.VMEM((2, slots * chunks // 2, LANES), BF16),
            pltpu.VMEM((tri, slots), BF16),
            pltpu.VMEM((slots, tri), BF16),
            pltpu.VMEM((rows, slots), BF16),
            pltpu.VMEM((slots, rows), BF16),
            pltpu.VMEM((rows, tri), BF16),
            pltpu.VMEM((1, rows), F32),
            pltpu.VMEM((1, rows), F32),
            pltpu.VMEM((tri, width), F32),
            pltpu.VMEM((tri, half), F32),
            pltpu.VMEM((tri, half), F32),
            pltpu.VMEM((tri, width), F32),
            pltpu.VMEM((2, rows, half), F32),
            pltpu.VMEM((2, hrows, half), BF16),
            pltpu.VMEM((2, hrows, half), BF16),
            pltpu.VMEM((2, 2, nz // 2, prow, half), BF16),
            pltpu.VMEM((2, 2, nz // 2, prow, half), BF16),
            pltpu.VMEM((2, rows, half), BF16),
            pltpu.VMEM((rows, 1), F32),
            pltpu.VMEM((slots * chunks // 2, LANES), F32),
            pltpu.VMEM((slots * chunks // 2, LANES), F32),
            pltpu.SemaphoreType.DMA((20,)),
            pltpu.SemaphoreType.DMA((8,)),
            pltpu.SemaphoreType.DMA((2, 2, nz // 2)),
            pltpu.SemaphoreType.DMA((2, 2, nz // 2)),
        ],
        compiler_params=pltpu.CompilerParams(
            collective_id=0, has_side_effects=True, vmem_limit_bytes=48 * 1024 * 1024
        ),
    )(*[pltpu.with_memory_space_constraint(a, pltpu.HBM) for a in (
        entity_table,
        adagrad_state.reshape(1, rows),
        relation_phase,
        head_owner.reshape(1, tri),
        head_row.reshape(1, tri),
        relation_id.reshape(1, tri),
        tail_row.reshape(1, tri),
        negative_row.reshape(1, negs),
    )])
    return new_table, new_state.reshape(rows)


def solution(mesh):
    return jax.shard_map(
        functools.partial(on_device, mesh.shape["ent"], mesh.shape["dp"]),
        mesh=mesh,
        in_specs=(
            P("ent", None),
            P("ent"),
            P(),
            P(("dp", "ent"), None),
            P(("dp", "ent")),
            P(("dp", "ent")),
            P(("dp", "ent")),
            P(("dp", "ent")),
        ),
        out_specs=(P("ent", None), P("ent")),
        check_vma=False,
    )
```

```python
import functools

import jax
import jax.numpy as jnp
from jax import lax
from jax.experimental import pallas as pl
from jax.experimental.pallas import tpu as pltpu
from jax.sharding import PartitionSpec as P

MARGIN = 12.0
LEARN_RATE = 0.25
F32 = jnp.float32
BF16 = jnp.bfloat16
LANES = 128


def onehot(condition):
    return jnp.where(condition, 1.0, 0.0).astype(BF16)


def iota(shape, dim):
    return lax.broadcasted_iota(jnp.int32, shape, dim)


def to_column(row):
    wide = jnp.broadcast_to(row, (LANES, row.shape[1]))
    return jnp.transpose(wide)[:, 0:1]


def to_row(column):
    wide = jnp.broadcast_to(column, (column.shape[0], LANES))
    return jnp.transpose(wide)[0:1, :]


def dot(a, b):
    return jnp.dot(a, b, preferred_element_type=F32)


def dot_nt(a, b, precision=None):
    return lax.dot_general(
        a, b, (((1,), (1,)), ((), ())), preferred_element_type=F32, precision=precision
    )


def split3(x):
    first = x.astype(BF16)
    rest = x - first.astype(F32)
    second = rest.astype(BF16)
    third = (rest - second.astype(F32)).astype(BF16)
    return first, second, third


def kernel(
    n_ent,
    n_dp,
    cap,
    table_hbm,
    state_hbm,
    phase_hbm,
    owner_hbm,
    hrow_hbm,
    rel_hbm,
    tail_hbm,
    neg_hbm,
    out_table,
    out_state,
    table,
    table_bf,
    phase,
    state_ref,
    owner_ref,
    hrow_ref,
    rel_ref,
    tail_ref,
    neg_ref,
    flat,
    req_send,
    req_recv,
    rep_send,
    rep_recv,
    gr_send,
    gr_recv,
    pick,
    pick_t,
    asked,
    asked_t,
    tail_hot,
    row_sq,
    count,
    positive,
    cosine,
    sine,
    rotated,
    partial,
    pair_send,
    pair_recv,
    ring_send,
    ring_recv,
    total,
    state_col,
    gr_flat_0,
    gr_flat_1,
    sems,
    load_sems,
    ring_sems,
    spread_sems,
):
    rows, width = table.shape
    half = width // 2
    gr_flat = (gr_flat_0, gr_flat_1)
    tri = hrow_ref.shape[1]
    negs = neg_ref.shape[1]
    rels = phase.shape[0]
    slots = n_ent * cap
    chunks = width // LANES
    blk = cap * chunks
    nz = n_dp // 2
    hrows = rows // 2
    prow = rows // n_dp
    ny = n_ent // 4 if n_ent > 4 else 2
    nx = n_ent // ny
    tile = 256
    tiles = width // tile

    ent = lax.axis_index("ent")
    dp = lax.axis_index("dp")
    z = lax.div(dp, 2)
    core = lax.rem(dp, 2)
    y = lax.div(ent, nx)
    x = lax.rem(ent, nx)
    partner = dp + 1 - 2 * core

    def shift(m, n):
        return ((m + 1) // 2 if m % 2 else -(m // 2)) % n

    def ent_peer(k):
        return lax.rem(y + shift(k % ny, ny), ny) * nx + lax.rem(x + k // ny, nx)

    def z_peer(k):
        return lax.rem(z + shift(nz - k, nz), nz)

    def remote(src, dst, send_sem, recv_sem, axis, index):
        return pltpu.make_async_remote_copy(
            src_ref=src,
            dst_ref=dst,
            send_sem=send_sem,
            recv_sem=recv_sem,
            device_id={axis: index},
            device_id_type=pl.DeviceIdType.MESH,
        )

    loads = [
        pltpu.make_async_copy(source, target, load_sems.at[i])
        for i, (source, target) in enumerate(
            (
                (owner_hbm, owner_ref),
                (hrow_hbm, hrow_ref),
                (table_hbm, table),
                (tail_hbm, tail_ref),
                (rel_hbm, rel_ref),
                (neg_hbm, neg_ref),
                (state_hbm, state_ref),
                (phase_hbm, phase),
            )
        )
    ]
    for load in loads:
        load.start()

    barrier = pltpu.get_barrier_semaphore()

    def greet(axis, index):
        pl.semaphore_signal(
            barrier, inc=1, device_id={axis: index}, device_id_type=pl.DeviceIdType.MESH
        )

    for k in range(1, n_ent):
        greet("ent", ent_peer(k))
    for k in range(1, nz):
        greet("dp", 2 * z_peer(k) + core)
    greet("dp", partner)

    loads[0].wait()
    loads[1].wait()
    owner_row = owner_ref[...]
    own_hot = owner_row == iota((n_ent, tri), 0)
    own_bf = onehot(own_hot)
    before = onehot(iota((tri, tri), 0) < iota((tri, tri), 1))
    prior = dot(own_bf, before)
    rank = jnp.sum(jnp.where(own_hot, prior, 0.0), axis=0, keepdims=True).astype(jnp.int32)
    slot_row = owner_row * cap + rank
    lane_row = lax.rem(ent * cap + rank, LANES)
    lane_hot = onehot(lane_row == iota((LANES, tri), 0))
    wanted = hrow_ref[...] + 1
    high = lax.shift_right_logical(wanted, 5)
    low = wanted - high * 32
    high_part = jnp.where(own_hot, high.astype(F32), 0.0).astype(BF16)
    low_part = jnp.where(own_hot, low.astype(F32), 0.0).astype(BF16)
    request = dot_nt(high_part, lane_hot) * 32.0 + dot_nt(low_part, lane_hot)
    for o in range(n_ent):
        req_send[o] = request[o : o + 1, :]

    pl.semaphore_wait(barrier, n_ent - 1 + nz - 1 + 1)

    for k in range(1, n_ent):
        q = ent_peer(k)
        remote(req_send.at[q], req_recv.at[ent], sems.at[0], sems.at[1], "ent", q).start()
    req_recv[ent] = req_send[ent]

    loads[2].wait()

    def cast_table(j, carry):
        columns = pl.ds(pl.multiple_of(j * tile, tile), tile)
        table_bf[:, columns] = table[:, columns].astype(BF16)
        return carry

    lax.fori_loop(0, tiles, cast_table, 0)

    most = pl.ds(0, n_ent - 1)
    got = remote(
        req_send.at[most], req_recv.at[most], sems.at[0], sems.at[1], "ent", ent_peer(1)
    )
    got.wait_recv()
    got.wait_send()

    inbox = jnp.concatenate([req_recv[o] for o in range(n_ent)], axis=0)
    first = iota((n_ent, LANES), 0) * cap
    lane = iota((n_ent, LANES), 1)
    offset = lax.rem(lane - first + LANES * n_ent, LANES)
    vreg = lax.shift_right_logical(first + offset, 7)
    ask_parts = []
    for v in range(-(-slots // LANES)):
        mine = jnp.logical_and(offset < cap, vreg == v)
        ask_parts.append(jnp.sum(jnp.where(mine, inbox, 0.0), axis=0, keepdims=True))
    ask_row = jnp.concatenate(ask_parts, axis=1)[:, :slots].astype(jnp.int32) - 1
    ask_col = to_column(ask_row)
    asked_t[...] = onehot(ask_col == iota((slots, rows), 1))

    def fetch(j, carry):
        columns = pl.ds(pl.multiple_of(j * tile, tile), tile)
        part = dot(asked_t[...], table_bf[:, columns])
        flat[pl.ds(2 * j, slots, stride=chunks), :] = part[:, :LANES]
        flat[pl.ds(2 * j + 1, slots, stride=chunks), :] = part[:, LANES:]
        return carry

    lax.fori_loop(0, tiles, fetch, 0)

    def pack_rows(buffer, source, target):
        size = buffer.shape[0] // n_ent

        def body(k, carry):
            block = pl.ds(pl.multiple_of(k * size, 16), size)
            source[block, :] = buffer[block, :].astype(BF16)
            return carry

        lax.fori_loop(0, n_ent, body, 0)
        own = pl.ds(pl.multiple_of(ent * size, 16), size)
        target[own, :] = buffer[own, :].astype(BF16)

    def start_rows(source, target, sem):
        size = target.shape[0] // n_ent
        own = pl.ds(pl.multiple_of(ent * size, 16), size)
        for k in range(1, n_ent):
            q = ent_peer(k)
            block = pl.ds(pl.multiple_of(q * size, 16), size)
            remote(
                source.at[block], target.at[own], sems.at[sem], sems.at[sem + 1], "ent", q
            ).start()

    def all_rows(source, target, sem):
        most = pl.ds(0, target.shape[0] // n_ent * (n_ent - 1))
        return remote(
            source.at[most], target.at[most], sems.at[sem], sems.at[sem + 1], "ent", ent_peer(1)
        )

    def unpack(target, buffer):
        size = buffer.shape[0] // n_ent

        def body(k, carry):
            block = pl.ds(pl.multiple_of(k * size, 16), size)
            buffer[block, :] = target[block, :].astype(F32)
            return carry

        lax.fori_loop(0, n_ent, body, 0)

    def slot_tile(j):
        return jnp.concatenate(
            [
                flat[pl.ds(2 * j, slots, stride=chunks), :],
                flat[pl.ds(2 * j + 1, slots, stride=chunks), :],
            ],
            axis=1,
        ).astype(BF16)

    pack_rows(flat, rep_send, rep_recv)
    start_rows(rep_send, rep_recv, 2)

    for load in loads[3:]:
        load.wait()
    asked[...] = onehot(ask_row == iota((rows, slots), 0))
    pick_t[...] = onehot(slot_row == iota((slots, tri), 0))
    pick[...] = onehot(to_column(slot_row) == iota((tri, slots), 1))

    neg = neg_ref[...]
    neg_high = lax.shift_right_logical(neg, 7)
    neg_low = neg - neg_high * LANES
    counts = dot_nt(
        onehot(neg_high == iota((8, negs), 0)), onehot(neg_low == iota((LANES, negs), 0))
    )
    count[...] = jnp.concatenate([counts[v : v + 1, :] for v in range(rows // LANES)], axis=1)

    tail_row = tail_ref[...]
    tail_hot[...] = onehot(tail_row == iota((rows, tri), 0))
    tail_pick = onehot(to_column(tail_row) == iota((tri, rows), 1))

    def tails(j, square):
        columns = pl.ds(pl.multiple_of(j * tile, tile), tile)
        part = table[:, columns]
        parts = split3(part)
        positive[:, columns] = (
            dot(tail_pick, parts[2]) + dot(tail_pick, parts[1]) + dot(tail_pick, parts[0])
        )
        return square + jnp.sum(part * part, axis=1, keepdims=True)

    row_sq[...] = to_row(lax.fori_loop(0, tiles, tails, jnp.zeros((rows, 1), F32)))

    rel_pick = onehot(to_column(rel_ref[...]) == iota((tri, rels), 1))

    def angles(j, carry):
        columns = pl.ds(pl.multiple_of(j * LANES, LANES), LANES)
        parts = split3(phase[:, columns])
        angle = dot(rel_pick, parts[2]) + dot(rel_pick, parts[1]) + dot(rel_pick, parts[0])
        cosine[:, columns] = jnp.cos(angle)
        sine[:, columns] = jnp.sin(angle)
        return carry

    lax.fori_loop(0, half // LANES, angles, 0)
    state_col[...] = to_column(state_ref[...])

    replies = all_rows(rep_send, rep_recv, 2)
    replies.wait_recv()
    replies.wait_send()
    unpack(rep_recv, flat)

    def rotate(j, sums):
        sums_rot, sums_diff = sums
        re = pl.ds(pl.multiple_of(j * tile, tile), tile)
        im = pl.ds(pl.multiple_of(half + j * tile, tile), tile)
        head_re = dot(pick[...], slot_tile(j))
        head_im = dot(pick[...], slot_tile(j + tiles // 2))
        cos, sin = cosine[:, re], sine[:, re]
        rot_re = head_re * cos - head_im * sin
        rot_im = head_re * sin + head_im * cos
        rotated[:, re] = rot_re
        rotated[:, im] = rot_im
        diff_re = rot_re - positive[:, re]
        diff_im = rot_im - positive[:, im]
        sums_rot += jnp.sum(rot_re * rot_re + rot_im * rot_im, axis=1, keepdims=True)
        sums_diff += jnp.sum(diff_re * diff_re + diff_im * diff_im, axis=1, keepdims=True)
        return sums_rot, sums_diff

    nothing = jnp.zeros((tri, 1), F32)
    rot_sq, diff_sq = lax.fori_loop(0, tiles // 2, rotate, (nothing, nothing))
    rotated_bf = rotated[...].astype(BF16)
    scores = dot_nt(rotated_bf, table_bf[...])
    distance = (rot_sq + row_sq[...] - 2.0 * scores) * (1.0 / half)
    dist_pos = diff_sq * (1.0 / half)
    logits = MARGIN - distance
    times = count[...]
    named = times > 0.0
    masked = jnp.where(named, logits, -jnp.inf)
    shifted = times * jnp.exp(masked - jnp.max(masked, axis=1, keepdims=True))
    weights = shifted / jnp.sum(shifted, axis=1, keepdims=True)
    row_coef = -0.5 * weights * jax.nn.sigmoid(logits)
    pos_coef = 0.5 * jax.nn.sigmoid(dist_pos - MARGIN)
    row_coef_bf = row_coef.astype(BF16)
    total_coef = pos_coef + jnp.sum(row_coef, axis=1, keepdims=True)

    quarter = half // 2
    for h in range(2):
        re = pl.ds(h * quarter, quarter)
        im = pl.ds(half + h * quarter, quarter)
        out = []
        for columns in (re, im):
            pulled = dot(row_coef_bf, table_bf[:, columns])
            out.append(
                2.0
                / half
                * (total_coef * rotated[:, columns] - pos_coef * positive[:, columns] - pulled)
            )
        cos, sin = cosine[:, re], sine[:, re]
        grad_re = (out[0] * cos + out[1] * sin).astype(BF16)
        grad_im = (out[1] * cos - out[0] * sin).astype(BF16)
        for at, value in ((0, grad_re), (2, grad_im)):
            part = dot(pick_t[...], value)
            gr_flat[h][pl.ds(at, slots, stride=4), :] = part[:, :LANES]
            gr_flat[h][pl.ds(at + 1, slots, stride=4), :] = part[:, LANES:]
        pack_rows(gr_flat[h], gr_send.at[h], gr_recv.at[h])
        if h == 0:
            start_rows(gr_send.at[h], gr_recv.at[h], 4)

    scale = 2.0 / half
    turned = jnp.transpose(row_coef)
    column = jnp.sum(turned, axis=1, keepdims=True) * scale
    turned_bf = turned.astype(BF16)
    pos_scaled = pos_coef * -scale

    def own_part(h):
        def body(part, carry):
            columns = pl.ds(pl.multiple_of(part * half + h * quarter, quarter), quarter)
            rot = rotated[:, columns]
            push = pos_scaled * (rot - positive[:, columns])
            push_high = push.astype(BF16)
            push_low = (push - push_high.astype(F32)).astype(BF16)
            partial[h, :, pl.ds(pl.multiple_of(part * quarter, quarter), quarter)] = (
                column * table[:, columns]
                - scale * dot(turned_bf, rot.astype(BF16))
                + dot(tail_hot[...], push_high)
                + dot(tail_hot[...], push_low)
            )
            return carry

        lax.fori_loop(0, 2, body, 0)

    theirs = pl.ds(pl.multiple_of((1 - core) * hrows, hrows), hrows)
    ours = pl.ds(pl.multiple_of(core * hrows, hrows), hrows)

    def rows_of(index):
        return pl.ds(pl.multiple_of(core * hrows + index * prow, prow), prow)

    def chip(distance):
        return lax.rem(z + distance + nz, nz)

    def part_of(w):
        return pl.ds(w * quarter, quarter)

    def add_incoming(h, some):
        def body(part, carry):
            columns = pl.ds(pl.multiple_of(part * quarter, quarter), quarter)
            value = jnp.concatenate(
                [
                    gr_flat[h][pl.ds(2 * part, slots, stride=4), :],
                    gr_flat[h][pl.ds(2 * part + 1, slots, stride=4), :],
                ],
                axis=1,
            ).astype(BF16)
            sums = partial[h, some, columns] + dot(asked[some, :], value)
            if some is theirs:
                pair_send[h, :, columns] = sums.astype(BF16)
            else:
                partial[h, some, columns] = sums
            return carry

        lax.fori_loop(0, 2, body, 0)

    def pair(h):
        return remote(
            pair_send.at[h], pair_recv.at[h], sems.at[8 + 2 * h], sems.at[9 + 2 * h], "dp", partner
        )

    def collect(h):
        all_rows(gr_send.at[h], gr_recv.at[h], 4 + 2 * h).wait_recv()
        unpack(gr_recv.at[h], gr_flat[h])
        add_incoming(h, theirs)
        pair(h).start()
        add_incoming(h, ours)

    def take_pair(h):
        pair(h).wait_recv()
        partial[h, ours, :] += pair_recv[h].astype(F32)

    steps = (1, -1)

    def ring(h, kind, w):
        source, target = ring_send.at[h, kind, w], ring_recv.at[h, kind, w]
        if kind == 0:
            source, target = source.at[:, part_of(w)], target.at[:, part_of(w)]
        return remote(
            source,
            target,
            sems.at[12 + h],
            ring_sems.at[h, kind, w],
            "dp",
            2 * chip(steps[w] * (2, 1, 1, 2)[kind]) + core,
        )

    def sum_first(h):
        for kind in range(3):
            for w in range(2):
                piece = rows_of(chip(steps[w] * (4, 3, 1)[kind]))
                columns = part_of(w) if kind == 0 else slice(None)
                ring_send[h, kind, w, :, columns] = partial[h, piece, columns].astype(BF16)
                ring(h, kind, w).start()

    def sum_second(h):
        for w in range(2):
            ring(h, 1, w).wait_recv()
            ring(h, 0, w).wait_recv()
            value = partial[h, rows_of(chip(2 * steps[w])), :] + ring_recv[h, 1, w].astype(F32)
            more = ring_recv[h, 0, w, :, part_of(w)].astype(F32)
            same = slice(w * quarter, (w + 1) * quarter)
            other = slice((1 - w) * quarter, (2 - w) * quarter)
            ring_send[h, 3, w, :, part_of(w)] = (value[:, same] + more).astype(BF16)
            ring_send[h, 3, w, :, part_of(1 - w)] = value[:, other].astype(BF16)
            ring(h, 3, w).start()

    def sum_end(h):
        value = partial[h, rows_of(z), :]
        for kind in (2, 3):
            for w in range(2):
                ring(h, kind, w).wait_recv()
                value += ring_recv[h, kind, w].astype(F32)
        total[h, rows_of(z), :] = value.astype(BF16)

    def spread(h, kind, w):
        begun = chip((0, 0, -2, -2)[kind] * steps[w])
        piece = total.at[h, rows_of(begun)]
        if kind == 3:
            piece = piece.at[:, part_of(w)]
        return remote(
            piece,
            piece,
            sems.at[14 + h],
            spread_sems.at[h, kind, w],
            "dp",
            2 * chip(steps[w] * (2, 1, 1, 2)[kind]) + core,
        )

    def across(h, piece):
        return remote(piece, piece, sems.at[16 + 2 * h], sems.at[17 + 2 * h], "dp", partner)

    def cross(h, distance):
        across(h, total.at[h, rows_of(chip(distance))]).start()

    def spread_first(h):
        for kind in (0, 1):
            for w in range(2):
                spread(h, kind, w).start()
        cross(h, 0)

    def spread_second(h):
        for w in range(2):
            spread(h, 0, w).wait_recv()
            spread(h, 2, w).start()
            spread(h, 3, w).start()
            cross(h, -2 * steps[w])

    def spread_end(h):
        for kind, distance in ((1, 1), (2, 3)):
            for w in range(2):
                spread(h, kind, w).wait_recv()
                cross(h, -distance * steps[w])
        for w in range(2):
            spread(h, 3, w).wait_recv()
        cross(h, 4)

    own_part(0)
    own_part(1)
    all_rows(gr_send.at[0], gr_recv.at[0], 4).wait_send()
    start_rows(gr_send.at[1], gr_recv.at[1], 6)
    collect(0)
    take_pair(0)
    sum_first(0)
    sum_second(0)
    sum_end(0)
    spread_first(0)
    collect(1)
    take_pair(1)
    sum_first(1)
    spread_second(0)
    sum_second(1)
    spread_end(0)
    sum_end(1)
    spread_first(1)
    spread_second(1)
    spread_end(1)

    def update(first_row):
        def body(k, carry):
            block = pl.ds(pl.multiple_of(first_row + k * 32, 32), 32)
            values = [total[h, block, :].astype(F32) for h in range(2)]
            square = values[0] * values[0] + values[1] * values[1]
            new = state_col[block, :] + jnp.sum(square, axis=1, keepdims=True) / width
            state_col[block, :] = new
            rate = LEARN_RATE / jnp.sqrt(new)
            for h in range(2):
                for part in range(2):
                    columns = pl.ds(part * half + h * quarter, quarter)
                    value = values[h][:, part * quarter : (part + 1) * quarter]
                    out_table[block, columns] = table[block, columns] - value * rate
            return carry

        lax.fori_loop(0, hrows // 32, body, 0)

    update(core * hrows)
    for h in range(2):
        across(h, total.at[h, theirs]).wait_recv()
    update((1 - core) * hrows)
    out_state[...] = to_row(state_col[...])
    all_rows(gr_send.at[1], gr_recv.at[1], 6).wait_send()
    for h in range(2):
        pair(h).wait_send()
        pieces = pl.ds(0, (nz - 1) * prow)
        piece = total.at[h, pieces]
        remote(piece, piece, sems.at[12 + h], sems.at[12 + h], "dp", partner).wait_send()
        remote(piece, piece, sems.at[14 + h], sems.at[14 + h], "dp", partner).wait_send()
        across(h, total.at[h, ours]).wait_send()


def on_device(
    n_ent,
    n_dp,
    entity_table,
    adagrad_state,
    relation_phase,
    head_owner,
    head_row,
    relation_id,
    tail_row,
    negative_row,
):
    rows, width = entity_table.shape
    rels, half = relation_phase.shape
    tri = head_row.shape[0]
    negs = negative_row.shape[0]
    cap = 12
    slots = n_ent * cap
    chunks = width // LANES
    hrows = rows // 2
    prow = rows // n_dp
    nz = n_dp // 2
    vmem = pl.BlockSpec(memory_space=pltpu.VMEM)
    hbm = pl.BlockSpec(memory_space=pltpu.HBM)
    new_table, new_state = pl.pallas_call(
        functools.partial(kernel, n_ent, n_dp, cap),
        out_shape=(
            jax.ShapeDtypeStruct((rows, width), F32),
            jax.ShapeDtypeStruct((1, rows), F32),
        ),
        in_specs=[hbm] * 8,
        out_specs=(vmem, vmem),
        scratch_shapes=[
            pltpu.VMEM((rows, width), F32),
            pltpu.VMEM((rows, width), BF16),
            pltpu.VMEM((rels, half), F32),
            pltpu.VMEM((1, rows), F32),
            pltpu.VMEM((1, tri), jnp.int32),
            pltpu.VMEM((1, tri), jnp.int32),
            pltpu.VMEM((1, tri), jnp.int32),
            pltpu.VMEM((1, tri), jnp.int32),
            pltpu.VMEM((1, negs), jnp.int32),
            pltpu.VMEM((slots * chunks, LANES), F32),
            pltpu.VMEM((n_ent, 1, LANES), F32),
            pltpu.VMEM((n_ent, 1, LANES), F32),
            pltpu.VMEM((slots * chunks, LANES), BF16),
            pltpu.VMEM((slots * chunks, LANES), BF16),
            pltpu.VMEM((2, slots * chunks // 2, LANES), BF16),
            pltpu.VMEM((2, slots * chunks // 2, LANES), BF16),
            pltpu.VMEM((tri, slots), BF16),
            pltpu.VMEM((slots, tri), BF16),
            pltpu.VMEM((rows, slots), BF16),
            pltpu.VMEM((slots, rows), BF16),
            pltpu.VMEM((rows, tri), BF16),
            pltpu.VMEM((1, rows), F32),
            pltpu.VMEM((1, rows), F32),
            pltpu.VMEM((tri, width), F32),
            pltpu.VMEM((tri, half), F32),
            pltpu.VMEM((tri, half), F32),
            pltpu.VMEM((tri, width), F32),
            pltpu.VMEM((2, rows, half), F32),
            pltpu.VMEM((2, hrows, half), BF16),
            pltpu.VMEM((2, hrows, half), BF16),
            pltpu.VMEM((2, 4, 2, prow, half), BF16),
            pltpu.VMEM((2, 4, 2, prow, half), BF16),
            pltpu.VMEM((2, rows, half), BF16),
            pltpu.VMEM((rows, 1), F32),
            pltpu.VMEM((slots * chunks // 2, LANES), F32),
            pltpu.VMEM((slots * chunks // 2, LANES), F32),
            pltpu.SemaphoreType.DMA((20,)),
            pltpu.SemaphoreType.DMA((8,)),
            pltpu.SemaphoreType.DMA((2, 4, 2)),
            pltpu.SemaphoreType.DMA((2, 4, 2)),
        ],
        compiler_params=pltpu.CompilerParams(
            collective_id=0, has_side_effects=True, vmem_limit_bytes=48 * 1024 * 1024
        ),
    )(*[pltpu.with_memory_space_constraint(a, pltpu.HBM) for a in (
        entity_table,
        adagrad_state.reshape(1, rows),
        relation_phase,
        head_owner.reshape(1, tri),
        head_row.reshape(1, tri),
        relation_id.reshape(1, tri),
        tail_row.reshape(1, tri),
        negative_row.reshape(1, negs),
    )])
    return new_table, new_state.reshape(rows)


def solution(mesh):
    return jax.shard_map(
        functools.partial(on_device, mesh.shape["ent"], mesh.shape["dp"]),
        mesh=mesh,
        in_specs=(
            P("ent", None),
            P("ent"),
            P(),
            P(("dp", "ent"), None),
            P(("dp", "ent")),
            P(("dp", "ent")),
            P(("dp", "ent")),
            P(("dp", "ent")),
        ),
        out_specs=(P("ent", None), P("ent")),
        check_vma=False,
    )
```

```python
import functools

import jax
import jax.numpy as jnp
from jax import lax
from jax.experimental import pallas as pl
from jax.experimental.pallas import tpu as pltpu
from jax.sharding import PartitionSpec as P

MARGIN = 12.0
LEARN_RATE = 0.25
F32 = jnp.float32
BF16 = jnp.bfloat16
LANES = 128


def onehot(condition):
    return jnp.where(condition, 1.0, 0.0).astype(BF16)


def iota(shape, dim):
    return lax.broadcasted_iota(jnp.int32, shape, dim)


def to_column(row):
    wide = jnp.broadcast_to(row, (LANES, row.shape[1]))
    return jnp.transpose(wide)[:, 0:1]


def to_row(column):
    wide = jnp.broadcast_to(column, (column.shape[0], LANES))
    return jnp.transpose(wide)[0:1, :]


def dot(a, b):
    return jnp.dot(a, b, preferred_element_type=F32)


def dot_nt(a, b, precision=None):
    return lax.dot_general(
        a, b, (((1,), (1,)), ((), ())), preferred_element_type=F32, precision=precision
    )


def split3(x):
    first = x.astype(BF16)
    rest = x - first.astype(F32)
    second = rest.astype(BF16)
    third = (rest - second.astype(F32)).astype(BF16)
    return first, second, third


def kernel(
    n_ent,
    n_dp,
    cap,
    table_hbm,
    state_hbm,
    phase_hbm,
    owner_hbm,
    hrow_hbm,
    rel_hbm,
    tail_hbm,
    neg_hbm,
    out_table,
    out_state,
    table,
    table_bf,
    phase,
    state_ref,
    owner_ref,
    hrow_ref,
    rel_ref,
    tail_ref,
    neg_ref,
    flat,
    req_send,
    req_recv,
    rep_send,
    rep_recv,
    gr_send,
    gr_recv,
    pick,
    pick_t,
    asked,
    asked_t,
    tail_hot,
    row_sq,
    count,
    positive,
    cosine,
    sine,
    rotated,
    partial,
    pair_send,
    pair_recv,
    ring_send,
    ring_recv,
    total,
    state_col,
    gr_flat_0,
    gr_flat_1,
    sems,
    load_sems,
    ring_sems,
    spread_sems,
    across_sems,
):
    rows, width = table.shape
    half = width // 2
    gr_flat = (gr_flat_0, gr_flat_1)
    tri = hrow_ref.shape[1]
    negs = neg_ref.shape[1]
    rels = phase.shape[0]
    slots = n_ent * cap
    chunks = width // LANES
    blk = cap * chunks
    nz = n_dp // 2
    hrows = rows // 2
    prow = rows // n_dp
    ny = n_ent // 4 if n_ent > 4 else 2
    nx = n_ent // ny
    tile = 256
    tiles = width // tile

    ent = lax.axis_index("ent")
    dp = lax.axis_index("dp")
    z = lax.div(dp, 2)
    core = lax.rem(dp, 2)
    y = lax.div(ent, nx)
    x = lax.rem(ent, nx)
    partner = dp + 1 - 2 * core

    def shift(m, n):
        return ((m + 1) // 2 if m % 2 else -(m // 2)) % n

    def ent_peer(k):
        return lax.rem(y + shift(k % ny, ny), ny) * nx + lax.rem(x + k // ny, nx)

    def z_peer(k):
        return lax.rem(z + shift(nz - k, nz), nz)

    def remote(src, dst, send_sem, recv_sem, axis, index):
        return pltpu.make_async_remote_copy(
            src_ref=src,
            dst_ref=dst,
            send_sem=send_sem,
            recv_sem=recv_sem,
            device_id={axis: index},
            device_id_type=pl.DeviceIdType.MESH,
        )

    loads = [
        pltpu.make_async_copy(source, target, load_sems.at[i])
        for i, (source, target) in enumerate(
            (
                (owner_hbm, owner_ref),
                (hrow_hbm, hrow_ref),
                (table_hbm, table),
                (tail_hbm, tail_ref),
                (rel_hbm, rel_ref),
                (neg_hbm, neg_ref),
                (state_hbm, state_ref),
                (phase_hbm, phase),
            )
        )
    ]
    for load in loads:
        load.start()

    barrier = pltpu.get_barrier_semaphore()

    def greet(axis, index):
        pl.semaphore_signal(
            barrier, inc=1, device_id={axis: index}, device_id_type=pl.DeviceIdType.MESH
        )

    for k in range(1, n_ent):
        greet("ent", ent_peer(k))
    for k in range(1, nz):
        greet("dp", 2 * z_peer(k) + core)
    greet("dp", partner)

    loads[0].wait()
    loads[1].wait()
    owner_row = owner_ref[...]
    own_hot = owner_row == iota((n_ent, tri), 0)
    own_bf = onehot(own_hot)
    before = onehot(iota((tri, tri), 0) < iota((tri, tri), 1))
    prior = dot(own_bf, before)
    rank = jnp.sum(jnp.where(own_hot, prior, 0.0), axis=0, keepdims=True).astype(jnp.int32)
    slot_row = owner_row * cap + rank
    lane_row = lax.rem(ent * cap + rank, LANES)
    lane_hot = onehot(lane_row == iota((LANES, tri), 0))
    wanted = hrow_ref[...] + 1
    high = lax.shift_right_logical(wanted, 5)
    low = wanted - high * 32
    high_part = jnp.where(own_hot, high.astype(F32), 0.0).astype(BF16)
    low_part = jnp.where(own_hot, low.astype(F32), 0.0).astype(BF16)
    request = dot_nt(high_part, lane_hot) * 32.0 + dot_nt(low_part, lane_hot)
    for o in range(n_ent):
        req_send[o] = request[o : o + 1, :]

    pl.semaphore_wait(barrier, n_ent - 1 + nz - 1 + 1)

    for k in range(1, n_ent):
        q = ent_peer(k)
        remote(req_send.at[q], req_recv.at[ent], sems.at[0], sems.at[1], "ent", q).start()
    req_recv[ent] = req_send[ent]

    loads[2].wait()

    def cast_table(j, carry):
        columns = pl.ds(pl.multiple_of(j * tile, tile), tile)
        table_bf[:, columns] = table[:, columns].astype(BF16)
        return carry

    lax.fori_loop(0, tiles, cast_table, 0)

    most = pl.ds(0, n_ent - 1)
    got = remote(
        req_send.at[most], req_recv.at[most], sems.at[0], sems.at[1], "ent", ent_peer(1)
    )
    got.wait_recv()
    got.wait_send()

    inbox = jnp.concatenate([req_recv[o] for o in range(n_ent)], axis=0)
    first = iota((n_ent, LANES), 0) * cap
    lane = iota((n_ent, LANES), 1)
    offset = lax.rem(lane - first + LANES * n_ent, LANES)
    vreg = lax.shift_right_logical(first + offset, 7)
    ask_parts = []
    for v in range(-(-slots // LANES)):
        mine = jnp.logical_and(offset < cap, vreg == v)
        ask_parts.append(jnp.sum(jnp.where(mine, inbox, 0.0), axis=0, keepdims=True))
    ask_row = jnp.concatenate(ask_parts, axis=1)[:, :slots].astype(jnp.int32) - 1
    ask_col = to_column(ask_row)
    asked_t[...] = onehot(ask_col == iota((slots, rows), 1))

    def fetch(j, carry):
        columns = pl.ds(pl.multiple_of(j * tile, tile), tile)
        part = dot(asked_t[...], table_bf[:, columns])
        flat[pl.ds(2 * j, slots, stride=chunks), :] = part[:, :LANES]
        flat[pl.ds(2 * j + 1, slots, stride=chunks), :] = part[:, LANES:]
        return carry

    lax.fori_loop(0, tiles, fetch, 0)

    def pack_rows(buffer, source, target):
        size = buffer.shape[0] // n_ent

        def body(k, carry):
            block = pl.ds(pl.multiple_of(k * size, 16), size)
            source[block, :] = buffer[block, :].astype(BF16)
            return carry

        lax.fori_loop(0, n_ent, body, 0)
        own = pl.ds(pl.multiple_of(ent * size, 16), size)
        target[own, :] = buffer[own, :].astype(BF16)

    def start_rows(source, target, sem):
        size = target.shape[0] // n_ent
        own = pl.ds(pl.multiple_of(ent * size, 16), size)
        for k in range(1, n_ent):
            q = ent_peer(k)
            block = pl.ds(pl.multiple_of(q * size, 16), size)
            remote(
                source.at[block], target.at[own], sems.at[sem], sems.at[sem + 1], "ent", q
            ).start()

    def all_rows(source, target, sem):
        most = pl.ds(0, target.shape[0] // n_ent * (n_ent - 1))
        return remote(
            source.at[most], target.at[most], sems.at[sem], sems.at[sem + 1], "ent", ent_peer(1)
        )

    def unpack(target, buffer):
        size = buffer.shape[0] // n_ent

        def body(k, carry):
            block = pl.ds(pl.multiple_of(k * size, 16), size)
            buffer[block, :] = target[block, :].astype(F32)
            return carry

        lax.fori_loop(0, n_ent, body, 0)

    def slot_tile(j):
        return jnp.concatenate(
            [
                flat[pl.ds(2 * j, slots, stride=chunks), :],
                flat[pl.ds(2 * j + 1, slots, stride=chunks), :],
            ],
            axis=1,
        ).astype(BF16)

    pack_rows(flat, rep_send, rep_recv)
    start_rows(rep_send, rep_recv, 2)

    for load in loads[3:]:
        load.wait()
    asked[...] = onehot(ask_row == iota((rows, slots), 0))
    pick_t[...] = onehot(slot_row == iota((slots, tri), 0))
    pick[...] = onehot(to_column(slot_row) == iota((tri, slots), 1))

    neg = neg_ref[...]
    neg_high = lax.shift_right_logical(neg, 7)
    neg_low = neg - neg_high * LANES
    counts = dot_nt(
        onehot(neg_high == iota((8, negs), 0)), onehot(neg_low == iota((LANES, negs), 0))
    )
    count[...] = jnp.concatenate([counts[v : v + 1, :] for v in range(rows // LANES)], axis=1)

    tail_row = tail_ref[...]
    tail_hot[...] = onehot(tail_row == iota((rows, tri), 0))
    tail_pick = onehot(to_column(tail_row) == iota((tri, rows), 1))

    def tails(j, square):
        columns = pl.ds(pl.multiple_of(j * tile, tile), tile)
        part = table[:, columns]
        parts = split3(part)
        positive[:, columns] = (
            dot(tail_pick, parts[2]) + dot(tail_pick, parts[1]) + dot(tail_pick, parts[0])
        )
        return square + jnp.sum(part * part, axis=1, keepdims=True)

    row_sq[...] = to_row(lax.fori_loop(0, tiles, tails, jnp.zeros((rows, 1), F32)))

    rel_pick = onehot(to_column(rel_ref[...]) == iota((tri, rels), 1))

    def angles(j, carry):
        columns = pl.ds(pl.multiple_of(j * LANES, LANES), LANES)
        parts = split3(phase[:, columns])
        angle = dot(rel_pick, parts[2]) + dot(rel_pick, parts[1]) + dot(rel_pick, parts[0])
        cosine[:, columns] = jnp.cos(angle)
        sine[:, columns] = jnp.sin(angle)
        return carry

    lax.fori_loop(0, half // LANES, angles, 0)
    state_col[...] = to_column(state_ref[...])

    replies = all_rows(rep_send, rep_recv, 2)
    replies.wait_recv()
    replies.wait_send()
    unpack(rep_recv, flat)

    def rotate(j, sums):
        sums_rot, sums_diff = sums
        re = pl.ds(pl.multiple_of(j * tile, tile), tile)
        im = pl.ds(pl.multiple_of(half + j * tile, tile), tile)
        head_re = dot(pick[...], slot_tile(j))
        head_im = dot(pick[...], slot_tile(j + tiles // 2))
        cos, sin = cosine[:, re], sine[:, re]
        rot_re = head_re * cos - head_im * sin
        rot_im = head_re * sin + head_im * cos
        rotated[:, re] = rot_re
        rotated[:, im] = rot_im
        diff_re = rot_re - positive[:, re]
        diff_im = rot_im - positive[:, im]
        sums_rot += jnp.sum(rot_re * rot_re + rot_im * rot_im, axis=1, keepdims=True)
        sums_diff += jnp.sum(diff_re * diff_re + diff_im * diff_im, axis=1, keepdims=True)
        return sums_rot, sums_diff

    nothing = jnp.zeros((tri, 1), F32)
    rot_sq, diff_sq = lax.fori_loop(0, tiles // 2, rotate, (nothing, nothing))
    rotated_bf = rotated[...].astype(BF16)
    scores = dot_nt(rotated_bf, table_bf[...])
    distance = (rot_sq + row_sq[...] - 2.0 * scores) * (1.0 / half)
    dist_pos = diff_sq * (1.0 / half)
    logits = MARGIN - distance
    times = count[...]
    named = times > 0.0
    masked = jnp.where(named, logits, -jnp.inf)
    shifted = times * jnp.exp(masked - jnp.max(masked, axis=1, keepdims=True))
    weights = shifted / jnp.sum(shifted, axis=1, keepdims=True)
    row_coef = -0.5 * weights * jax.nn.sigmoid(logits)
    pos_coef = 0.5 * jax.nn.sigmoid(dist_pos - MARGIN)
    row_coef_bf = row_coef.astype(BF16)
    total_coef = pos_coef + jnp.sum(row_coef, axis=1, keepdims=True)

    quarter = half // 2
    for h in range(2):
        re = pl.ds(h * quarter, quarter)
        im = pl.ds(half + h * quarter, quarter)
        out = []
        for columns in (re, im):
            pulled = dot(row_coef_bf, table_bf[:, columns])
            out.append(
                2.0
                / half
                * (total_coef * rotated[:, columns] - pos_coef * positive[:, columns] - pulled)
            )
        cos, sin = cosine[:, re], sine[:, re]
        grad_re = (out[0] * cos + out[1] * sin).astype(BF16)
        grad_im = (out[1] * cos - out[0] * sin).astype(BF16)
        for at, value in ((0, grad_re), (2, grad_im)):
            part = dot(pick_t[...], value)
            gr_flat[h][pl.ds(at, slots, stride=4), :] = part[:, :LANES]
            gr_flat[h][pl.ds(at + 1, slots, stride=4), :] = part[:, LANES:]
        pack_rows(gr_flat[h], gr_send.at[h], gr_recv.at[h])
        if h == 0:
            start_rows(gr_send.at[h], gr_recv.at[h], 4)

    scale = 2.0 / half
    turned = jnp.transpose(row_coef)
    column = jnp.sum(turned, axis=1, keepdims=True) * scale
    turned_bf = turned.astype(BF16)
    pos_scaled = pos_coef * -scale

    def own_part(h):
        def body(part, carry):
            columns = pl.ds(pl.multiple_of(part * half + h * quarter, quarter), quarter)
            rot = rotated[:, columns]
            push = pos_scaled * (rot - positive[:, columns])
            push_high = push.astype(BF16)
            push_low = (push - push_high.astype(F32)).astype(BF16)
            partial[h, :, pl.ds(pl.multiple_of(part * quarter, quarter), quarter)] = (
                column * table[:, columns]
                - scale * dot(turned_bf, rot.astype(BF16))
                + dot(tail_hot[...], push_high)
                + dot(tail_hot[...], push_low)
            )
            return carry

        lax.fori_loop(0, 2, body, 0)

    theirs = pl.ds(pl.multiple_of((1 - core) * hrows, hrows), hrows)
    ours = pl.ds(pl.multiple_of(core * hrows, hrows), hrows)

    def rows_of(index):
        return pl.ds(pl.multiple_of(core * hrows + index * prow, prow), prow)

    def chip(distance):
        return lax.rem(z + distance + nz, nz)

    def part_of(w):
        return pl.ds(w * quarter, quarter)

    def add_incoming(h, some):
        def body(part, carry):
            columns = pl.ds(pl.multiple_of(part * quarter, quarter), quarter)
            value = jnp.concatenate(
                [
                    gr_flat[h][pl.ds(2 * part, slots, stride=4), :],
                    gr_flat[h][pl.ds(2 * part + 1, slots, stride=4), :],
                ],
                axis=1,
            ).astype(BF16)
            sums = partial[h, some, columns] + dot(asked[some, :], value)
            if some is theirs:
                pair_send[h, :, columns] = sums.astype(BF16)
            else:
                partial[h, some, columns] = sums
            return carry

        lax.fori_loop(0, 2, body, 0)

    def pair(h):
        return remote(
            pair_send.at[h], pair_recv.at[h], sems.at[8 + 2 * h], sems.at[9 + 2 * h], "dp", partner
        )

    def collect(h):
        all_rows(gr_send.at[h], gr_recv.at[h], 4 + 2 * h).wait_recv()
        unpack(gr_recv.at[h], gr_flat[h])
        add_incoming(h, theirs)
        pair(h).start()
        add_incoming(h, ours)

    def take_pair(h):
        pair(h).wait_recv()
        partial[h, ours, :] += pair_recv[h].astype(F32)

    steps = (1, -1)

    def ring(h, kind, w):
        source, target = ring_send.at[h, kind, w], ring_recv.at[h, kind, w]
        if kind == 0:
            source, target = source.at[:, part_of(w)], target.at[:, part_of(w)]
        return remote(
            source,
            target,
            sems.at[12 + h],
            ring_sems.at[h, kind, w],
            "dp",
            2 * chip(steps[w] * (2, 1, 1, 2)[kind]) + core,
        )

    def sum_first(h):
        for kind in range(3):
            for w in range(2):
                piece = rows_of(chip(steps[w] * (4, 3, 1)[kind]))
                columns = part_of(w) if kind == 0 else slice(None)
                ring_send[h, kind, w, :, columns] = partial[h, piece, columns].astype(BF16)
                ring(h, kind, w).start()

    def sum_second(h):
        for w in range(2):
            ring(h, 1, w).wait_recv()
            ring(h, 0, w).wait_recv()
            value = partial[h, rows_of(chip(2 * steps[w])), :] + ring_recv[h, 1, w].astype(F32)
            more = ring_recv[h, 0, w, :, part_of(w)].astype(F32)
            same = slice(w * quarter, (w + 1) * quarter)
            other = slice((1 - w) * quarter, (2 - w) * quarter)
            ring_send[h, 3, w, :, part_of(w)] = (value[:, same] + more).astype(BF16)
            ring_send[h, 3, w, :, part_of(1 - w)] = value[:, other].astype(BF16)
            ring(h, 3, w).start()

    def sum_end(h):
        value = partial[h, rows_of(z), :]
        for kind in (2, 3):
            for w in range(2):
                ring(h, kind, w).wait_recv()
                value += ring_recv[h, kind, w].astype(F32)
        total[h, rows_of(z), :] = value.astype(BF16)

    def spread(h, kind, w):
        begun = chip((0, 0, -2, -2)[kind] * steps[w])
        piece = total.at[h, rows_of(begun)]
        if kind == 3:
            piece = piece.at[:, part_of(w)]
        return remote(
            piece,
            piece,
            sems.at[14 + h],
            spread_sems.at[h, kind, w],
            "dp",
            2 * chip(steps[w] * (2, 1, 1, 2)[kind]) + core,
        )

    def across(h, distance, side):
        half_rows = (core + side - 2 * core * side) * hrows
        piece = total.at[
            h, pl.ds(pl.multiple_of(half_rows + chip(distance) * prow, prow), prow)
        ]
        return remote(
            piece, piece, sems.at[16 + h], across_sems.at[h, distance + 3], "dp", partner
        )

    def cross(h, distance):
        across(h, distance, 0).start()

    def spread_first(h):
        for kind in (0, 1):
            for w in range(2):
                spread(h, kind, w).start()
        cross(h, 0)

    def spread_second(h):
        for w in range(2):
            spread(h, 0, w).wait_recv()
            spread(h, 2, w).start()
            spread(h, 3, w).start()
            cross(h, -2 * steps[w])

    def spread_near(h):
        for w in range(2):
            spread(h, 1, w).wait_recv()
            cross(h, -steps[w])

    def spread_far(h):
        for w in range(2):
            spread(h, 2, w).wait_recv()
            cross(h, -3 * steps[w])
        for w in range(2):
            spread(h, 3, w).wait_recv()
        cross(h, 4)

    def update(distance, side):
        if side == 1:
            for h in range(2):
                across(h, distance, 1).wait_recv()
        half_rows = (core + side - 2 * core * side) * hrows
        block = pl.ds(pl.multiple_of(half_rows + chip(distance) * prow, prow), prow)
        values = [total[h, block, :].astype(F32) for h in range(2)]
        square = values[0] * values[0] + values[1] * values[1]
        new = state_col[block, :] + jnp.sum(square, axis=1, keepdims=True) / width
        state_col[block, :] = new
        rate = LEARN_RATE / jnp.sqrt(new)
        for h in range(2):
            for part in range(2):
                columns = pl.ds(part * half + h * quarter, quarter)
                value = values[h][:, part * quarter : (part + 1) * quarter]
                out_table[block, columns] = table[block, columns] - value * rate

    own_part(0)
    own_part(1)
    all_rows(gr_send.at[0], gr_recv.at[0], 4).wait_send()
    start_rows(gr_send.at[1], gr_recv.at[1], 6)
    collect(0)
    take_pair(0)
    sum_first(0)
    sum_second(0)
    collect(1)
    sum_end(0)
    spread_first(0)
    take_pair(1)
    sum_first(1)
    spread_second(0)
    sum_second(1)
    spread_near(0)
    sum_end(1)
    spread_first(1)
    spread_far(0)
    spread_second(1)
    spread_near(1)
    for side in range(2):
        for distance in (0, 2, -2, 1, -1):
            update(distance, side)
    spread_far(1)
    for side in range(2):
        for distance in (3, -3, 4):
            update(distance, side)
    out_state[...] = to_row(state_col[...])
    all_rows(gr_send.at[1], gr_recv.at[1], 6).wait_send()
    for h in range(2):
        pair(h).wait_send()
        pieces = total.at[h, pl.ds(0, (nz - 1) * prow)]
        remote(pieces, pieces, sems.at[12 + h], sems.at[12 + h], "dp", partner).wait_send()
        remote(pieces, pieces, sems.at[14 + h], sems.at[14 + h], "dp", partner).wait_send()
        pieces = total.at[h, ours]
        remote(pieces, pieces, sems.at[16 + h], sems.at[16 + h], "dp", partner).wait_send()


def on_device(
    n_ent,
    n_dp,
    entity_table,
    adagrad_state,
    relation_phase,
    head_owner,
    head_row,
    relation_id,
    tail_row,
    negative_row,
):
    rows, width = entity_table.shape
    rels, half = relation_phase.shape
    tri = head_row.shape[0]
    negs = negative_row.shape[0]
    cap = 12
    slots = n_ent * cap
    chunks = width // LANES
    hrows = rows // 2
    prow = rows // n_dp
    nz = n_dp // 2
    vmem = pl.BlockSpec(memory_space=pltpu.VMEM)
    hbm = pl.BlockSpec(memory_space=pltpu.HBM)
    new_table, new_state = pl.pallas_call(
        functools.partial(kernel, n_ent, n_dp, cap),
        out_shape=(
            jax.ShapeDtypeStruct((rows, width), F32),
            jax.ShapeDtypeStruct((1, rows), F32),
        ),
        in_specs=[hbm] * 8,
        out_specs=(vmem, vmem),
        scratch_shapes=[
            pltpu.VMEM((rows, width), F32),
            pltpu.VMEM((rows, width), BF16),
            pltpu.VMEM((rels, half), F32),
            pltpu.VMEM((1, rows), F32),
            pltpu.VMEM((1, tri), jnp.int32),
            pltpu.VMEM((1, tri), jnp.int32),
            pltpu.VMEM((1, tri), jnp.int32),
            pltpu.VMEM((1, tri), jnp.int32),
            pltpu.VMEM((1, negs), jnp.int32),
            pltpu.VMEM((slots * chunks, LANES), F32),
            pltpu.VMEM((n_ent, 1, LANES), F32),
            pltpu.VMEM((n_ent, 1, LANES), F32),
            pltpu.VMEM((slots * chunks, LANES), BF16),
            pltpu.VMEM((slots * chunks, LANES), BF16),
            pltpu.VMEM((2, slots * chunks // 2, LANES), BF16),
            pltpu.VMEM((2, slots * chunks // 2, LANES), BF16),
            pltpu.VMEM((tri, slots), BF16),
            pltpu.VMEM((slots, tri), BF16),
            pltpu.VMEM((rows, slots), BF16),
            pltpu.VMEM((slots, rows), BF16),
            pltpu.VMEM((rows, tri), BF16),
            pltpu.VMEM((1, rows), F32),
            pltpu.VMEM((1, rows), F32),
            pltpu.VMEM((tri, width), F32),
            pltpu.VMEM((tri, half), F32),
            pltpu.VMEM((tri, half), F32),
            pltpu.VMEM((tri, width), F32),
            pltpu.VMEM((2, rows, half), F32),
            pltpu.VMEM((2, hrows, half), BF16),
            pltpu.VMEM((2, hrows, half), BF16),
            pltpu.VMEM((2, 4, 2, prow, half), BF16),
            pltpu.VMEM((2, 4, 2, prow, half), BF16),
            pltpu.VMEM((2, rows, half), BF16),
            pltpu.VMEM((rows, 1), F32),
            pltpu.VMEM((slots * chunks // 2, LANES), F32),
            pltpu.VMEM((slots * chunks // 2, LANES), F32),
            pltpu.SemaphoreType.DMA((20,)),
            pltpu.SemaphoreType.DMA((8,)),
            pltpu.SemaphoreType.DMA((2, 4, 2)),
            pltpu.SemaphoreType.DMA((2, 4, 2)),
            pltpu.SemaphoreType.DMA((2, 8)),
        ],
        compiler_params=pltpu.CompilerParams(
            collective_id=0, has_side_effects=True, vmem_limit_bytes=48 * 1024 * 1024
        ),
    )(*[pltpu.with_memory_space_constraint(a, pltpu.HBM) for a in (
        entity_table,
        adagrad_state.reshape(1, rows),
        relation_phase,
        head_owner.reshape(1, tri),
        head_row.reshape(1, tri),
        relation_id.reshape(1, tri),
        tail_row.reshape(1, tri),
        negative_row.reshape(1, negs),
    )])
    return new_table, new_state.reshape(rows)


def solution(mesh):
    return jax.shard_map(
        functools.partial(on_device, mesh.shape["ent"], mesh.shape["dp"]),
        mesh=mesh,
        in_specs=(
            P("ent", None),
            P("ent"),
            P(),
            P(("dp", "ent"), None),
            P(("dp", "ent")),
            P(("dp", "ent")),
            P(("dp", "ent")),
            P(("dp", "ent")),
        ),
        out_specs=(P("ent", None), P("ent")),
        check_vma=False,
    )
```

```python
import functools

import jax
import jax.numpy as jnp
from jax import lax
from jax.experimental import pallas as pl
from jax.experimental.pallas import tpu as pltpu
from jax.sharding import PartitionSpec as P

MARGIN = 12.0
LEARN_RATE = 0.25
F32 = jnp.float32
BF16 = jnp.bfloat16
LANES = 128


def onehot(condition):
    return jnp.where(condition, 1.0, 0.0).astype(BF16)


def iota(shape, dim):
    return lax.broadcasted_iota(jnp.int32, shape, dim)


def to_column(row):
    wide = jnp.broadcast_to(row, (LANES, row.shape[1]))
    return jnp.transpose(wide)[:, 0:1]


def to_row(column):
    wide = jnp.broadcast_to(column, (column.shape[0], LANES))
    return jnp.transpose(wide)[0:1, :]


def dot(a, b):
    return jnp.dot(a, b, preferred_element_type=F32)


def dot_nt(a, b, precision=None):
    return lax.dot_general(
        a, b, (((1,), (1,)), ((), ())), preferred_element_type=F32, precision=precision
    )


def split3(x):
    first = x.astype(BF16)
    rest = x - first.astype(F32)
    second = rest.astype(BF16)
    third = (rest - second.astype(F32)).astype(BF16)
    return first, second, third


def kernel(
    n_ent,
    n_dp,
    cap,
    table_hbm,
    state_hbm,
    phase_hbm,
    owner_hbm,
    hrow_hbm,
    rel_hbm,
    tail_hbm,
    neg_hbm,
    out_table,
    out_state,
    table,
    table_bf,
    phase,
    state_ref,
    owner_ref,
    hrow_ref,
    rel_ref,
    tail_ref,
    neg_ref,
    req_send,
    req_recv,
    rep_send,
    rep_recv,
    gr_send,
    gr_recv,
    pick,
    pick_t,
    asked,
    asked_t,
    tail_hot,
    row_sq,
    count,
    positive,
    cosine,
    sine,
    rotated,
    partial,
    pair_send,
    pair_recv,
    ring_send,
    ring_recv,
    total,
    state_col,
    gr_flat_0,
    gr_flat_1,
    sems,
    load_sems,
    ring_sems,
    spread_sems,
    across_sems,
):
    rows, width = table.shape
    half = width // 2
    gr_flat = (gr_flat_0, gr_flat_1)
    tri = hrow_ref.shape[1]
    negs = neg_ref.shape[1]
    rels = phase.shape[0]
    slots = n_ent * cap
    chunks = width // LANES
    blk = cap * chunks
    nz = n_dp // 2
    hrows = rows // 2
    prow = rows // n_dp
    ny = n_ent // 4 if n_ent > 4 else 2
    nx = n_ent // ny
    tile = 256
    tiles = width // tile

    ent = lax.axis_index("ent")
    dp = lax.axis_index("dp")
    z = lax.div(dp, 2)
    core = lax.rem(dp, 2)
    y = lax.div(ent, nx)
    x = lax.rem(ent, nx)
    partner = dp + 1 - 2 * core

    def shift(m, n):
        return ((m + 1) // 2 if m % 2 else -(m // 2)) % n

    def hops(k):
        dy, dx = shift(k % ny, ny), k // ny
        return min(dy, ny - dy) + min(dx, nx - dx)

    far_first = sorted(range(1, n_ent), key=hops, reverse=True)

    def ent_peer(k):
        return lax.rem(y + shift(k % ny, ny), ny) * nx + lax.rem(x + k // ny, nx)

    def z_peer(k):
        return lax.rem(z + shift(nz - k, nz), nz)

    def remote(src, dst, send_sem, recv_sem, axis, index):
        return pltpu.make_async_remote_copy(
            src_ref=src,
            dst_ref=dst,
            send_sem=send_sem,
            recv_sem=recv_sem,
            device_id={axis: index},
            device_id_type=pl.DeviceIdType.MESH,
        )

    loads = [
        pltpu.make_async_copy(source, target, load_sems.at[i])
        for i, (source, target) in enumerate(
            (
                (owner_hbm, owner_ref),
                (hrow_hbm, hrow_ref),
                (table_hbm, table),
                (tail_hbm, tail_ref),
                (rel_hbm, rel_ref),
                (neg_hbm, neg_ref),
                (state_hbm, state_ref),
                (phase_hbm, phase),
            )
        )
    ]
    for load in loads:
        load.start()

    barrier = pltpu.get_barrier_semaphore()

    def greet(axis, index):
        pl.semaphore_signal(
            barrier, inc=1, device_id={axis: index}, device_id_type=pl.DeviceIdType.MESH
        )

    for k in far_first:
        greet("ent", ent_peer(k))
    for k in range(1, nz):
        greet("dp", 2 * z_peer(k) + core)
    greet("dp", partner)

    loads[0].wait()
    loads[1].wait()
    owner_row = owner_ref[...]
    own_hot = owner_row == iota((n_ent, tri), 0)
    own_bf = onehot(own_hot)
    before = onehot(iota((tri, tri), 0) < iota((tri, tri), 1))
    prior = dot(own_bf, before)
    rank = jnp.sum(jnp.where(own_hot, prior, 0.0), axis=0, keepdims=True).astype(jnp.int32)
    slot_row = owner_row * cap + rank
    lane_row = lax.rem(ent * cap + rank, LANES)
    lane_hot = onehot(lane_row == iota((LANES, tri), 0))
    wanted = hrow_ref[...] + 1
    high = lax.shift_right_logical(wanted, 5)
    low = wanted - high * 32
    high_part = jnp.where(own_hot, high.astype(F32), 0.0).astype(BF16)
    low_part = jnp.where(own_hot, low.astype(F32), 0.0).astype(BF16)
    request = dot_nt(high_part, lane_hot) * 32.0 + dot_nt(low_part, lane_hot)
    for o in range(n_ent):
        req_send[o] = request[o : o + 1, :]

    pl.semaphore_wait(barrier, n_ent - 1 + nz - 1 + 1)

    for k in far_first:
        q = ent_peer(k)
        remote(req_send.at[q], req_recv.at[ent], sems.at[0], sems.at[1], "ent", q).start()
    req_recv[ent] = req_send[ent]

    loads[2].wait()

    def cast_table(j, carry):
        columns = pl.ds(pl.multiple_of(j * tile, tile), tile)
        table_bf[:, columns] = table[:, columns].astype(BF16)
        return carry

    lax.fori_loop(0, tiles, cast_table, 0)

    most = pl.ds(0, n_ent - 1)
    got = remote(
        req_send.at[most], req_recv.at[most], sems.at[0], sems.at[1], "ent", ent_peer(1)
    )
    got.wait_recv()
    got.wait_send()

    inbox = jnp.concatenate([req_recv[o] for o in range(n_ent)], axis=0)
    first = iota((n_ent, LANES), 0) * cap
    lane = iota((n_ent, LANES), 1)
    offset = lax.rem(lane - first + LANES * n_ent, LANES)
    vreg = lax.shift_right_logical(first + offset, 7)
    ask_parts = []
    for v in range(-(-slots // LANES)):
        mine = jnp.logical_and(offset < cap, vreg == v)
        ask_parts.append(jnp.sum(jnp.where(mine, inbox, 0.0), axis=0, keepdims=True))
    ask_row = jnp.concatenate(ask_parts, axis=1)[:, :slots].astype(jnp.int32) - 1
    ask_col = to_column(ask_row)
    asked_t[...] = onehot(ask_col == iota((slots, rows), 1))

    def fetch(h):
        for part in range(2):
            columns = pl.ds(part * half + h * tile, tile)
            value = dot(asked_t[...], table_bf[:, columns])
            gr_flat[h][pl.ds(2 * part, slots, stride=4), :] = value[:, :LANES]
            gr_flat[h][pl.ds(2 * part + 1, slots, stride=4), :] = value[:, LANES:]

    def pack_rows(buffer, source, target):
        size = buffer.shape[0] // n_ent

        def body(k, carry):
            block = pl.ds(pl.multiple_of(k * size, 16), size)
            source[block, :] = buffer[block, :].astype(BF16)
            return carry

        lax.fori_loop(0, n_ent, body, 0)
        own = pl.ds(pl.multiple_of(ent * size, 16), size)
        target[own, :] = buffer[own, :].astype(BF16)

    def start_rows(source, target, sem):
        size = target.shape[0] // n_ent
        own = pl.ds(pl.multiple_of(ent * size, 16), size)
        for k in far_first:
            q = ent_peer(k)
            block = pl.ds(pl.multiple_of(q * size, 16), size)
            remote(
                source.at[block], target.at[own], sems.at[sem], sems.at[sem + 1], "ent", q
            ).start()

    def all_rows(source, target, sem):
        most = pl.ds(0, target.shape[0] // n_ent * (n_ent - 1))
        return remote(
            source.at[most], target.at[most], sems.at[sem], sems.at[sem + 1], "ent", ent_peer(1)
        )

    def unpack(target, buffer):
        size = buffer.shape[0] // n_ent

        def body(k, carry):
            block = pl.ds(pl.multiple_of(k * size, 16), size)
            buffer[block, :] = target[block, :].astype(F32)
            return carry

        lax.fori_loop(0, n_ent, body, 0)

    def slot_tile(h, part):
        return jnp.concatenate(
            [
                gr_flat[h][pl.ds(2 * part, slots, stride=4), :],
                gr_flat[h][pl.ds(2 * part + 1, slots, stride=4), :],
            ],
            axis=1,
        ).astype(BF16)

    for h in range(2):
        fetch(h)
        pack_rows(gr_flat[h], rep_send.at[h], rep_recv.at[h])
        if h == 0:
            start_rows(rep_send.at[h], rep_recv.at[h], 2)

    for load in loads[3:]:
        load.wait()
    asked[...] = onehot(ask_row == iota((rows, slots), 0))
    pick_t[...] = onehot(slot_row == iota((slots, tri), 0))
    pick[...] = onehot(to_column(slot_row) == iota((tri, slots), 1))

    neg = neg_ref[...]
    neg_high = lax.shift_right_logical(neg, 7)
    neg_low = neg - neg_high * LANES
    counts = dot_nt(
        onehot(neg_high == iota((8, negs), 0)), onehot(neg_low == iota((LANES, negs), 0))
    )
    count[...] = jnp.concatenate([counts[v : v + 1, :] for v in range(rows // LANES)], axis=1)

    tail_row = tail_ref[...]
    tail_hot[...] = onehot(tail_row == iota((rows, tri), 0))
    tail_pick = onehot(to_column(tail_row) == iota((tri, rows), 1))

    def tails(j, square):
        columns = pl.ds(pl.multiple_of(j * tile, tile), tile)
        part = table[:, columns]
        parts = split3(part)
        positive[:, columns] = (
            dot(tail_pick, parts[2]) + dot(tail_pick, parts[1]) + dot(tail_pick, parts[0])
        )
        return square + jnp.sum(part * part, axis=1, keepdims=True)

    row_sq[...] = to_row(lax.fori_loop(0, tiles, tails, jnp.zeros((rows, 1), F32)))

    all_rows(rep_send.at[0], rep_recv.at[0], 2).wait_send()
    start_rows(rep_send.at[1], rep_recv.at[1], 18)
    rel_pick = onehot(to_column(rel_ref[...]) == iota((tri, rels), 1))

    def angles(j, carry):
        columns = pl.ds(pl.multiple_of(j * LANES, LANES), LANES)
        parts = split3(phase[:, columns])
        angle = dot(rel_pick, parts[2]) + dot(rel_pick, parts[1]) + dot(rel_pick, parts[0])
        cosine[:, columns] = jnp.cos(angle)
        sine[:, columns] = jnp.sin(angle)
        return carry

    lax.fori_loop(0, half // LANES, angles, 0)
    state_col[...] = to_column(state_ref[...])

    rot_sq = jnp.zeros((tri, 1), F32)
    diff_sq = jnp.zeros((tri, 1), F32)
    scores = jnp.zeros((tri, rows), F32)
    for h in range(2):
        all_rows(rep_send.at[h], rep_recv.at[h], (2, 18)[h]).wait_recv()
        unpack(rep_recv.at[h], gr_flat[h])
        re = pl.ds(h * tile, tile)
        im = pl.ds(half + h * tile, tile)
        head_re = dot(pick[...], slot_tile(h, 0))
        head_im = dot(pick[...], slot_tile(h, 1))
        cos, sin = cosine[:, re], sine[:, re]
        rot_re = head_re * cos - head_im * sin
        rot_im = head_re * sin + head_im * cos
        rotated[:, re] = rot_re
        rotated[:, im] = rot_im
        diff_re = rot_re - positive[:, re]
        diff_im = rot_im - positive[:, im]
        rot_sq += jnp.sum(rot_re * rot_re + rot_im * rot_im, axis=1, keepdims=True)
        diff_sq += jnp.sum(diff_re * diff_re + diff_im * diff_im, axis=1, keepdims=True)
        scores += dot_nt(rot_re.astype(BF16), table_bf[:, re])
        scores += dot_nt(rot_im.astype(BF16), table_bf[:, im])
    all_rows(rep_send.at[1], rep_recv.at[1], 18).wait_send()
    distance = (rot_sq + row_sq[...] - 2.0 * scores) * (1.0 / half)
    dist_pos = diff_sq * (1.0 / half)
    logits = MARGIN - distance
    times = count[...]
    named = times > 0.0
    masked = jnp.where(named, logits, -jnp.inf)
    shifted = times * jnp.exp(masked - jnp.max(masked, axis=1, keepdims=True))
    weights = shifted / jnp.sum(shifted, axis=1, keepdims=True)
    row_coef = -0.5 * weights * jax.nn.sigmoid(logits)
    pos_coef = 0.5 * jax.nn.sigmoid(dist_pos - MARGIN)
    row_coef_bf = row_coef.astype(BF16)
    total_coef = pos_coef + jnp.sum(row_coef, axis=1, keepdims=True)

    quarter = half // 2
    for h in range(2):
        re = pl.ds(h * quarter, quarter)
        im = pl.ds(half + h * quarter, quarter)
        out = []
        for columns in (re, im):
            pulled = dot(row_coef_bf, table_bf[:, columns])
            out.append(
                2.0
                / half
                * (total_coef * rotated[:, columns] - pos_coef * positive[:, columns] - pulled)
            )
        cos, sin = cosine[:, re], sine[:, re]
        grad_re = (out[0] * cos + out[1] * sin).astype(BF16)
        grad_im = (out[1] * cos - out[0] * sin).astype(BF16)
        for at, value in ((0, grad_re), (2, grad_im)):
            part = dot(pick_t[...], value)
            gr_flat[h][pl.ds(at, slots, stride=4), :] = part[:, :LANES]
            gr_flat[h][pl.ds(at + 1, slots, stride=4), :] = part[:, LANES:]
        pack_rows(gr_flat[h], gr_send.at[h], gr_recv.at[h])
        if h == 0:
            start_rows(gr_send.at[h], gr_recv.at[h], 4)

    scale = 2.0 / half
    turned = jnp.transpose(row_coef)
    column = jnp.sum(turned, axis=1, keepdims=True) * scale
    turned_bf = turned.astype(BF16)
    pos_scaled = pos_coef * -scale

    def own_part(h):
        def body(part, carry):
            columns = pl.ds(pl.multiple_of(part * half + h * quarter, quarter), quarter)
            rot = rotated[:, columns]
            push = pos_scaled * (rot - positive[:, columns])
            push_high = push.astype(BF16)
            push_low = (push - push_high.astype(F32)).astype(BF16)
            partial[h, :, pl.ds(pl.multiple_of(part * quarter, quarter), quarter)] = (
                column * table[:, columns]
                - scale * dot(turned_bf, rot.astype(BF16))
                + dot(tail_hot[...], push_high)
                + dot(tail_hot[...], push_low)
            )
            return carry

        lax.fori_loop(0, 2, body, 0)

    theirs = pl.ds(pl.multiple_of((1 - core) * hrows, hrows), hrows)
    ours = pl.ds(pl.multiple_of(core * hrows, hrows), hrows)

    def rows_of(index):
        return pl.ds(pl.multiple_of(core * hrows + index * prow, prow), prow)

    def chip(distance):
        return lax.rem(z + distance + nz, nz)

    def part_of(w):
        return pl.ds(w * quarter, quarter)

    def add_incoming(h, some):
        for part in range(2):
            columns = pl.ds(part * quarter, quarter)
            value = slot_tile(h, part)
            sums = partial[h, some, columns] + dot(asked[some, :], value)
            if some is theirs:
                pair_send[h, :, columns] = sums.astype(BF16)
            else:
                partial[h, some, columns] = sums

    def pair(h):
        return remote(
            pair_send.at[h], pair_recv.at[h], sems.at[8 + 2 * h], sems.at[9 + 2 * h], "dp", partner
        )

    def collect(h):
        all_rows(gr_send.at[h], gr_recv.at[h], 4 + 2 * h).wait_recv()
        unpack(gr_recv.at[h], gr_flat[h])
        add_incoming(h, theirs)
        pair(h).start()
        add_incoming(h, ours)

    def take_pair(h):
        pair(h).wait_recv()
        partial[h, ours, :] += pair_recv[h].astype(F32)

    steps = (1, -1)

    def ring(h, kind, w):
        source, target = ring_send.at[h, kind, w], ring_recv.at[h, kind, w]
        if kind == 0:
            source, target = source.at[:, part_of(w)], target.at[:, part_of(w)]
        return remote(
            source,
            target,
            sems.at[12 + h],
            ring_sems.at[h, kind, w],
            "dp",
            2 * chip(steps[w] * (2, 1, 1, 2)[kind]) + core,
        )

    def sum_first(h):
        for kind in range(3):
            for w in range(2):
                piece = rows_of(chip(steps[w] * (4, 3, 1)[kind]))
                columns = part_of(w) if kind == 0 else slice(None)
                ring_send[h, kind, w, :, columns] = partial[h, piece, columns].astype(BF16)
                ring(h, kind, w).start()

    def sum_second(h):
        for w in range(2):
            ring(h, 1, w).wait_recv()
            ring(h, 0, w).wait_recv()
            value = partial[h, rows_of(chip(2 * steps[w])), :] + ring_recv[h, 1, w].astype(F32)
            more = ring_recv[h, 0, w, :, part_of(w)].astype(F32)
            same = slice(w * quarter, (w + 1) * quarter)
            other = slice((1 - w) * quarter, (2 - w) * quarter)
            ring_send[h, 3, w, :, part_of(w)] = (value[:, same] + more).astype(BF16)
            ring_send[h, 3, w, :, part_of(1 - w)] = value[:, other].astype(BF16)
            ring(h, 3, w).start()

    def sum_end(h):
        value = partial[h, rows_of(z), :]
        for kind in (2, 3):
            for w in range(2):
                ring(h, kind, w).wait_recv()
                value += ring_recv[h, kind, w].astype(F32)
        total[h, rows_of(z), :] = value.astype(BF16)

    def spread(h, kind, w):
        begun = chip((0, 0, -2, -2)[kind] * steps[w])
        piece = total.at[h, rows_of(begun)]
        if kind == 3:
            piece = piece.at[:, part_of(w)]
        return remote(
            piece,
            piece,
            sems.at[14 + h],
            spread_sems.at[h, kind, w],
            "dp",
            2 * chip(steps[w] * (2, 1, 1, 2)[kind]) + core,
        )

    def across(h, distance, side):
        half_rows = (core + side - 2 * core * side) * hrows
        piece = total.at[
            h, pl.ds(pl.multiple_of(half_rows + chip(distance) * prow, prow), prow)
        ]
        return remote(
            piece, piece, sems.at[16 + h], across_sems.at[h, distance + 3], "dp", partner
        )

    def cross(h, distance):
        across(h, distance, 0).start()

    def spread_first(h):
        for kind in (0, 1):
            for w in range(2):
                spread(h, kind, w).start()
        cross(h, 0)

    def spread_second(h):
        for w in range(2):
            spread(h, 0, w).wait_recv()
            spread(h, 2, w).start()
            spread(h, 3, w).start()
            cross(h, -2 * steps[w])

    def spread_near(h):
        for w in range(2):
            spread(h, 1, w).wait_recv()
            cross(h, -steps[w])

    def spread_far(h):
        for w in range(2):
            spread(h, 2, w).wait_recv()
            cross(h, -3 * steps[w])
        for w in range(2):
            spread(h, 3, w).wait_recv()
        cross(h, 4)

    def update(distance, side):
        if side == 1:
            for h in range(2):
                across(h, distance, 1).wait_recv()
        half_rows = (core + side - 2 * core * side) * hrows
        block = pl.ds(pl.multiple_of(half_rows + chip(distance) * prow, prow), prow)
        values = [total[h, block, :].astype(F32) for h in range(2)]
        square = values[0] * values[0] + values[1] * values[1]
        new = state_col[block, :] + jnp.sum(square, axis=1, keepdims=True) / width
        state_col[block, :] = new
        rate = LEARN_RATE / jnp.sqrt(new)
        for h in range(2):
            for part in range(2):
                columns = pl.ds(part * half + h * quarter, quarter)
                value = values[h][:, part * quarter : (part + 1) * quarter]
                out_table[block, columns] = table[block, columns] - value * rate

    own_part(0)
    own_part(1)
    all_rows(gr_send.at[0], gr_recv.at[0], 4).wait_send()
    start_rows(gr_send.at[1], gr_recv.at[1], 6)
    collect(0)
    take_pair(0)
    sum_first(0)
    sum_second(0)
    collect(1)
    sum_end(0)
    spread_first(0)
    take_pair(1)
    sum_first(1)
    spread_second(0)
    sum_second(1)
    spread_near(0)
    sum_end(1)
    spread_first(1)
    spread_far(0)
    spread_second(1)
    spread_near(1)
    for side in range(2):
        for distance in (0, 2, -2, 1, -1):
            update(distance, side)
    spread_far(1)
    for side in range(2):
        for distance in (3, -3, 4):
            update(distance, side)
    out_state[...] = to_row(state_col[...])
    all_rows(gr_send.at[1], gr_recv.at[1], 6).wait_send()
    for h in range(2):
        pair(h).wait_send()
        pieces = total.at[h, pl.ds(0, (nz - 1) * prow)]
        remote(pieces, pieces, sems.at[12 + h], sems.at[12 + h], "dp", partner).wait_send()
        remote(pieces, pieces, sems.at[14 + h], sems.at[14 + h], "dp", partner).wait_send()
        pieces = total.at[h, ours]
        remote(pieces, pieces, sems.at[16 + h], sems.at[16 + h], "dp", partner).wait_send()


def on_device(
    n_ent,
    n_dp,
    entity_table,
    adagrad_state,
    relation_phase,
    head_owner,
    head_row,
    relation_id,
    tail_row,
    negative_row,
):
    rows, width = entity_table.shape
    rels, half = relation_phase.shape
    tri = head_row.shape[0]
    negs = negative_row.shape[0]
    cap = 12
    slots = n_ent * cap
    chunks = width // LANES
    hrows = rows // 2
    prow = rows // n_dp
    nz = n_dp // 2
    vmem = pl.BlockSpec(memory_space=pltpu.VMEM)
    hbm = pl.BlockSpec(memory_space=pltpu.HBM)
    new_table, new_state = pl.pallas_call(
        functools.partial(kernel, n_ent, n_dp, cap),
        out_shape=(
            jax.ShapeDtypeStruct((rows, width), F32),
            jax.ShapeDtypeStruct((1, rows), F32),
        ),
        in_specs=[hbm] * 8,
        out_specs=(vmem, vmem),
        scratch_shapes=[
            pltpu.VMEM((rows, width), F32),
            pltpu.VMEM((rows, width), BF16),
            pltpu.VMEM((rels, half), F32),
            pltpu.VMEM((1, rows), F32),
            pltpu.VMEM((1, tri), jnp.int32),
            pltpu.VMEM((1, tri), jnp.int32),
            pltpu.VMEM((1, tri), jnp.int32),
            pltpu.VMEM((1, tri), jnp.int32),
            pltpu.VMEM((1, negs), jnp.int32),
            pltpu.VMEM((n_ent, 1, LANES), F32),
            pltpu.VMEM((n_ent, 1, LANES), F32),
            pltpu.VMEM((2, slots * chunks // 2, LANES), BF16),
            pltpu.VMEM((2, slots * chunks // 2, LANES), BF16),
            pltpu.VMEM((2, slots * chunks // 2, LANES), BF16),
            pltpu.VMEM((2, slots * chunks // 2, LANES), BF16),
            pltpu.VMEM((tri, slots), BF16),
            pltpu.VMEM((slots, tri), BF16),
            pltpu.VMEM((rows, slots), BF16),
            pltpu.VMEM((slots, rows), BF16),
            pltpu.VMEM((rows, tri), BF16),
            pltpu.VMEM((1, rows), F32),
            pltpu.VMEM((1, rows), F32),
            pltpu.VMEM((tri, width), F32),
            pltpu.VMEM((tri, half), F32),
            pltpu.VMEM((tri, half), F32),
            pltpu.VMEM((tri, width), F32),
            pltpu.VMEM((2, rows, half), F32),
            pltpu.VMEM((2, hrows, half), BF16),
            pltpu.VMEM((2, hrows, half), BF16),
            pltpu.VMEM((2, 4, 2, prow, half), BF16),
            pltpu.VMEM((2, 4, 2, prow, half), BF16),
            pltpu.VMEM((2, rows, half), BF16),
            pltpu.VMEM((rows, 1), F32),
            pltpu.VMEM((slots * chunks // 2, LANES), F32),
            pltpu.VMEM((slots * chunks // 2, LANES), F32),
            pltpu.SemaphoreType.DMA((20,)),
            pltpu.SemaphoreType.DMA((8,)),
            pltpu.SemaphoreType.DMA((2, 4, 2)),
            pltpu.SemaphoreType.DMA((2, 4, 2)),
            pltpu.SemaphoreType.DMA((2, 8)),
        ],
        compiler_params=pltpu.CompilerParams(
            collective_id=0, has_side_effects=True, vmem_limit_bytes=48 * 1024 * 1024
        ),
    )(*[pltpu.with_memory_space_constraint(a, pltpu.HBM) for a in (
        entity_table,
        adagrad_state.reshape(1, rows),
        relation_phase,
        head_owner.reshape(1, tri),
        head_row.reshape(1, tri),
        relation_id.reshape(1, tri),
        tail_row.reshape(1, tri),
        negative_row.reshape(1, negs),
    )])
    return new_table, new_state.reshape(rows)


def solution(mesh):
    return jax.shard_map(
        functools.partial(on_device, mesh.shape["ent"], mesh.shape["dp"]),
        mesh=mesh,
        in_specs=(
            P("ent", None),
            P("ent"),
            P(),
            P(("dp", "ent"), None),
            P(("dp", "ent")),
            P(("dp", "ent")),
            P(("dp", "ent")),
            P(("dp", "ent")),
        ),
        out_specs=(P("ent", None), P("ent")),
        check_vma=False,
    )
```

```python
import functools

import jax
import jax.numpy as jnp
from jax import lax
from jax.experimental import pallas as pl
from jax.experimental.pallas import tpu as pltpu
from jax.sharding import PartitionSpec as P

MARGIN = 12.0
LEARN_RATE = 0.25
F32 = jnp.float32
BF16 = jnp.bfloat16
LANES = 128


def onehot(condition):
    return jnp.where(condition, 1.0, 0.0).astype(BF16)


def iota(shape, dim):
    return lax.broadcasted_iota(jnp.int32, shape, dim)


def to_column(row):
    wide = jnp.broadcast_to(row, (LANES, row.shape[1]))
    return jnp.transpose(wide)[:, 0:1]


def to_row(column):
    wide = jnp.broadcast_to(column, (column.shape[0], LANES))
    return jnp.transpose(wide)[0:1, :]


def dot(a, b):
    return jnp.dot(a, b, preferred_element_type=F32)


def dot_nt(a, b, precision=None):
    return lax.dot_general(
        a, b, (((1,), (1,)), ((), ())), preferred_element_type=F32, precision=precision
    )


def split3(x):
    first = x.astype(BF16)
    rest = x - first.astype(F32)
    second = rest.astype(BF16)
    third = (rest - second.astype(F32)).astype(BF16)
    return first, second, third


def kernel(
    n_ent,
    n_dp,
    cap,
    table_hbm,
    state_hbm,
    phase_hbm,
    owner_hbm,
    hrow_hbm,
    rel_hbm,
    tail_hbm,
    neg_hbm,
    out_table,
    out_state,
    table,
    table_bf,
    phase,
    state_ref,
    owner_ref,
    hrow_ref,
    rel_ref,
    tail_ref,
    neg_ref,
    req_send,
    req_recv,
    rep_send,
    rep_recv,
    gr_send,
    gr_recv,
    pick,
    pick_t,
    asked,
    asked_t,
    tail_hot,
    row_sq,
    count,
    positive,
    cosine,
    sine,
    rotated,
    partial,
    pair_send,
    pair_recv,
    ring_send,
    ring_recv,
    total,
    state_col,
    gr_flat_0,
    gr_flat_1,
    sems,
    load_sems,
    ring_sems,
    spread_sems,
    across_sems,
):
    rows, width = table.shape
    half = width // 2
    gr_flat = (gr_flat_0, gr_flat_1)
    tri = hrow_ref.shape[1]
    negs = neg_ref.shape[1]
    rels = phase.shape[0]
    slots = n_ent * cap
    chunks = width // LANES
    blk = cap * chunks
    nz = n_dp // 2
    hrows = rows // 2
    prow = rows // n_dp
    ny = n_ent // 4 if n_ent > 4 else 2
    nx = n_ent // ny
    tile = 256
    tiles = width // tile

    ent = lax.axis_index("ent")
    dp = lax.axis_index("dp")
    z = lax.div(dp, 2)
    core = lax.rem(dp, 2)
    y = lax.div(ent, nx)
    x = lax.rem(ent, nx)
    partner = dp + 1 - 2 * core

    def shift(m, n):
        return ((m + 1) // 2 if m % 2 else -(m // 2)) % n

    def hops(k):
        dy, dx = shift(k % ny, ny), k // ny
        return min(dy, ny - dy) + min(dx, nx - dx)

    far_first = sorted(range(1, n_ent), key=hops, reverse=True)

    def ent_peer(k):
        return lax.rem(y + shift(k % ny, ny), ny) * nx + lax.rem(x + k // ny, nx)

    def z_peer(k):
        return lax.rem(z + shift(nz - k, nz), nz)

    def remote(src, dst, send_sem, recv_sem, axis, index):
        return pltpu.make_async_remote_copy(
            src_ref=src,
            dst_ref=dst,
            send_sem=send_sem,
            recv_sem=recv_sem,
            device_id={axis: index},
            device_id_type=pl.DeviceIdType.MESH,
        )

    loads = [
        pltpu.make_async_copy(source, target, load_sems.at[i])
        for i, (source, target) in enumerate(
            (
                (owner_hbm, owner_ref),
                (hrow_hbm, hrow_ref),
                (table_hbm, table),
                (tail_hbm, tail_ref),
                (rel_hbm, rel_ref),
                (neg_hbm, neg_ref),
                (state_hbm, state_ref),
                (phase_hbm, phase),
            )
        )
    ]

    barrier = pltpu.get_barrier_semaphore()

    def greet(axis, index):
        pl.semaphore_signal(
            barrier, inc=1, device_id={axis: index}, device_id_type=pl.DeviceIdType.MESH
        )

    for k in far_first:
        greet("ent", ent_peer(k))
    for k in range(1, nz):
        greet("dp", 2 * z_peer(k) + core)
    greet("dp", partner)
    for load in loads:
        load.start()

    loads[0].wait()
    loads[1].wait()
    owner_row = owner_ref[...]
    own_hot = owner_row == iota((n_ent, tri), 0)
    own_bf = onehot(own_hot)
    before = onehot(iota((tri, tri), 0) < iota((tri, tri), 1))
    prior = dot(own_bf, before)
    rank = jnp.sum(jnp.where(own_hot, prior, 0.0), axis=0, keepdims=True).astype(jnp.int32)
    slot_row = owner_row * cap + rank
    lane_row = lax.rem(ent * cap + rank, LANES)
    lane_hot = onehot(lane_row == iota((LANES, tri), 0))
    wanted = hrow_ref[...] + 1
    high = lax.shift_right_logical(wanted, 5)
    low = wanted - high * 32
    high_part = jnp.where(own_hot, high.astype(F32), 0.0).astype(BF16)
    low_part = jnp.where(own_hot, low.astype(F32), 0.0).astype(BF16)
    request = dot_nt(high_part, lane_hot) * 32.0 + dot_nt(low_part, lane_hot)
    for o in range(n_ent):
        req_send[o] = request[o : o + 1, :]

    pl.semaphore_wait(barrier, n_ent - 1 + nz - 1 + 1)

    for k in far_first:
        q = ent_peer(k)
        remote(req_send.at[q], req_recv.at[ent], sems.at[0], sems.at[1], "ent", q).start()
    req_recv[ent] = req_send[ent]

    loads[2].wait()

    def cast_table(j, carry):
        columns = pl.ds(pl.multiple_of(j * tile, tile), tile)
        table_bf[:, columns] = table[:, columns].astype(BF16)
        return carry

    lax.fori_loop(0, tiles, cast_table, 0)

    most = pl.ds(0, n_ent - 1)
    got = remote(
        req_send.at[most], req_recv.at[most], sems.at[0], sems.at[1], "ent", ent_peer(1)
    )
    got.wait_recv()
    got.wait_send()

    inbox = jnp.concatenate([req_recv[o] for o in range(n_ent)], axis=0)
    first = iota((n_ent, LANES), 0) * cap
    lane = iota((n_ent, LANES), 1)
    offset = lax.rem(lane - first + LANES * n_ent, LANES)
    vreg = lax.shift_right_logical(first + offset, 7)
    ask_parts = []
    for v in range(-(-slots // LANES)):
        mine = jnp.logical_and(offset < cap, vreg == v)
        ask_parts.append(jnp.sum(jnp.where(mine, inbox, 0.0), axis=0, keepdims=True))
    ask_row = jnp.concatenate(ask_parts, axis=1)[:, :slots].astype(jnp.int32) - 1
    ask_col = to_column(ask_row)
    asked_t[...] = onehot(ask_col == iota((slots, rows), 1))

    def fetch(h):
        for part in range(2):
            columns = pl.ds(part * half + h * tile, tile)
            value = dot(asked_t[...], table_bf[:, columns])
            gr_flat[h][pl.ds(2 * part, slots, stride=4), :] = value[:, :LANES]
            gr_flat[h][pl.ds(2 * part + 1, slots, stride=4), :] = value[:, LANES:]

    def pack_rows(buffer, source, target):
        size = buffer.shape[0] // n_ent

        def body(k, carry):
            block = pl.ds(pl.multiple_of(k * size, 16), size)
            source[block, :] = buffer[block, :].astype(BF16)
            return carry

        lax.fori_loop(0, n_ent, body, 0)
        own = pl.ds(pl.multiple_of(ent * size, 16), size)
        target[own, :] = buffer[own, :].astype(BF16)

    def start_rows(source, target, sem):
        size = target.shape[0] // n_ent
        own = pl.ds(pl.multiple_of(ent * size, 16), size)
        for k in far_first:
            q = ent_peer(k)
            block = pl.ds(pl.multiple_of(q * size, 16), size)
            remote(
                source.at[block], target.at[own], sems.at[sem], sems.at[sem + 1], "ent", q
            ).start()

    def all_rows(source, target, sem):
        most = pl.ds(0, target.shape[0] // n_ent * (n_ent - 1))
        return remote(
            source.at[most], target.at[most], sems.at[sem], sems.at[sem + 1], "ent", ent_peer(1)
        )

    def unpack(target, buffer):
        size = buffer.shape[0] // n_ent

        def body(k, carry):
            block = pl.ds(pl.multiple_of(k * size, 16), size)
            buffer[block, :] = target[block, :].astype(F32)
            return carry

        lax.fori_loop(0, n_ent, body, 0)

    def slot_tile(h, part):
        return jnp.concatenate(
            [
                gr_flat[h][pl.ds(2 * part, slots, stride=4), :],
                gr_flat[h][pl.ds(2 * part + 1, slots, stride=4), :],
            ],
            axis=1,
        ).astype(BF16)

    for h in range(2):
        fetch(h)
        pack_rows(gr_flat[h], rep_send.at[h], rep_recv.at[h])
        if h == 0:
            start_rows(rep_send.at[h], rep_recv.at[h], 2)

    for load in loads[3:]:
        load.wait()
    asked[...] = onehot(ask_row == iota((rows, slots), 0))
    pick_t[...] = onehot(slot_row == iota((slots, tri), 0))
    pick[...] = onehot(to_column(slot_row) == iota((tri, slots), 1))

    neg = neg_ref[...]
    neg_high = lax.shift_right_logical(neg, 7)
    neg_low = neg - neg_high * LANES
    counts = dot_nt(
        onehot(neg_high == iota((8, negs), 0)), onehot(neg_low == iota((LANES, negs), 0))
    )
    count[...] = jnp.concatenate([counts[v : v + 1, :] for v in range(rows // LANES)], axis=1)

    tail_row = tail_ref[...]
    tail_hot[...] = onehot(tail_row == iota((rows, tri), 0))
    tail_pick = onehot(to_column(tail_row) == iota((tri, rows), 1))

    def tails(j, square):
        columns = pl.ds(pl.multiple_of(j * tile, tile), tile)
        part = table[:, columns]
        parts = split3(part)
        positive[:, columns] = (
            dot(tail_pick, parts[2]) + dot(tail_pick, parts[1]) + dot(tail_pick, parts[0])
        )
        return square + jnp.sum(part * part, axis=1, keepdims=True)

    row_sq[...] = to_row(lax.fori_loop(0, tiles, tails, jnp.zeros((rows, 1), F32)))

    all_rows(rep_send.at[0], rep_recv.at[0], 2).wait_send()
    start_rows(rep_send.at[1], rep_recv.at[1], 18)
    rel_pick = onehot(to_column(rel_ref[...]) == iota((tri, rels), 1))

    def angles(j, carry):
        columns = pl.ds(pl.multiple_of(j * LANES, LANES), LANES)
        parts = split3(phase[:, columns])
        angle = dot(rel_pick, parts[2]) + dot(rel_pick, parts[1]) + dot(rel_pick, parts[0])
        cosine[:, columns] = jnp.cos(angle)
        sine[:, columns] = jnp.sin(angle)
        return carry

    lax.fori_loop(0, half // LANES, angles, 0)
    state_col[...] = to_column(state_ref[...])

    rot_sq = jnp.zeros((tri, 1), F32)
    diff_sq = jnp.zeros((tri, 1), F32)
    scores = jnp.zeros((tri, rows), F32)
    for h in range(2):
        all_rows(rep_send.at[h], rep_recv.at[h], (2, 18)[h]).wait_recv()
        unpack(rep_recv.at[h], gr_flat[h])
        re = pl.ds(h * tile, tile)
        im = pl.ds(half + h * tile, tile)
        head_re = dot(pick[...], slot_tile(h, 0))
        head_im = dot(pick[...], slot_tile(h, 1))
        cos, sin = cosine[:, re], sine[:, re]
        rot_re = head_re * cos - head_im * sin
        rot_im = head_re * sin + head_im * cos
        rotated[:, re] = rot_re
        rotated[:, im] = rot_im
        diff_re = rot_re - positive[:, re]
        diff_im = rot_im - positive[:, im]
        rot_sq += jnp.sum(rot_re * rot_re + rot_im * rot_im, axis=1, keepdims=True)
        diff_sq += jnp.sum(diff_re * diff_re + diff_im * diff_im, axis=1, keepdims=True)
        scores += dot_nt(rot_re.astype(BF16), table_bf[:, re])
        scores += dot_nt(rot_im.astype(BF16), table_bf[:, im])
    all_rows(rep_send.at[1], rep_recv.at[1], 18).wait_send()
    distance = (rot_sq + row_sq[...] - 2.0 * scores) * (1.0 / half)
    dist_pos = diff_sq * (1.0 / half)
    logits = MARGIN - distance
    times = count[...]
    named = times > 0.0
    masked = jnp.where(named, logits, -jnp.inf)
    shifted = times * jnp.exp(masked - jnp.max(masked, axis=1, keepdims=True))
    weights = shifted / jnp.sum(shifted, axis=1, keepdims=True)
    row_coef = -0.5 * weights * jax.nn.sigmoid(logits)
    pos_coef = 0.5 * jax.nn.sigmoid(dist_pos - MARGIN)
    row_coef_bf = row_coef.astype(BF16)
    total_coef = pos_coef + jnp.sum(row_coef, axis=1, keepdims=True)

    quarter = half // 2
    for h in range(2):
        re = pl.ds(h * quarter, quarter)
        im = pl.ds(half + h * quarter, quarter)
        out = []
        for columns in (re, im):
            pulled = dot(row_coef_bf, table_bf[:, columns])
            out.append(
                2.0
                / half
                * (total_coef * rotated[:, columns] - pos_coef * positive[:, columns] - pulled)
            )
        cos, sin = cosine[:, re], sine[:, re]
        grad_re = (out[0] * cos + out[1] * sin).astype(BF16)
        grad_im = (out[1] * cos - out[0] * sin).astype(BF16)
        for at, value in ((0, grad_re), (2, grad_im)):
            part = dot(pick_t[...], value)
            gr_flat[h][pl.ds(at, slots, stride=4), :] = part[:, :LANES]
            gr_flat[h][pl.ds(at + 1, slots, stride=4), :] = part[:, LANES:]
        pack_rows(gr_flat[h], gr_send.at[h], gr_recv.at[h])
        if h == 0:
            start_rows(gr_send.at[h], gr_recv.at[h], 4)

    scale = 2.0 / half
    turned = jnp.transpose(row_coef)
    column = jnp.sum(turned, axis=1, keepdims=True) * scale
    turned_bf = turned.astype(BF16)
    pos_scaled = pos_coef * -scale

    def own_part(h):
        def body(part, carry):
            columns = pl.ds(pl.multiple_of(part * half + h * quarter, quarter), quarter)
            rot = rotated[:, columns]
            push = pos_scaled * (rot - positive[:, columns])
            push_high = push.astype(BF16)
            push_low = (push - push_high.astype(F32)).astype(BF16)
            partial[h, :, pl.ds(pl.multiple_of(part * quarter, quarter), quarter)] = (
                column * table[:, columns]
                - scale * dot(turned_bf, rot.astype(BF16))
                + dot(tail_hot[...], push_high)
                + dot(tail_hot[...], push_low)
            )
            return carry

        lax.fori_loop(0, 2, body, 0)

    theirs = pl.ds(pl.multiple_of((1 - core) * hrows, hrows), hrows)
    ours = pl.ds(pl.multiple_of(core * hrows, hrows), hrows)

    def rows_of(index):
        return pl.ds(pl.multiple_of(core * hrows + index * prow, prow), prow)

    def chip(distance):
        return lax.rem(z + distance + nz, nz)

    def part_of(w):
        return pl.ds(w * quarter, quarter)

    def add_incoming(h, some):
        for part in range(2):
            columns = pl.ds(part * quarter, quarter)
            value = slot_tile(h, part)
            sums = partial[h, some, columns] + dot(asked[some, :], value)
            if some is theirs:
                pair_send[h, :, columns] = sums.astype(BF16)
            else:
                partial[h, some, columns] = sums

    def pair(h):
        return remote(
            pair_send.at[h], pair_recv.at[h], sems.at[8 + 2 * h], sems.at[9 + 2 * h], "dp", partner
        )

    def collect(h):
        all_rows(gr_send.at[h], gr_recv.at[h], 4 + 2 * h).wait_recv()
        unpack(gr_recv.at[h], gr_flat[h])
        add_incoming(h, theirs)
        pair(h).start()
        add_incoming(h, ours)

    def take_pair(h):
        pair(h).wait_recv()
        partial[h, ours, :] += pair_recv[h].astype(F32)

    steps = (1, -1)

    def ring(h, kind, w):
        source, target = ring_send.at[h, kind, w], ring_recv.at[h, kind, w]
        if kind == 0:
            source, target = source.at[:, part_of(w)], target.at[:, part_of(w)]
        return remote(
            source,
            target,
            sems.at[12 + h],
            ring_sems.at[h, kind, w],
            "dp",
            2 * chip(steps[w] * (2, 1, 1, 2)[kind]) + core,
        )

    def sum_first(h):
        for kind in range(3):
            for w in range(2):
                piece = rows_of(chip(steps[w] * (4, 3, 1)[kind]))
                columns = part_of(w) if kind == 0 else slice(None)
                ring_send[h, kind, w, :, columns] = partial[h, piece, columns].astype(BF16)
                ring(h, kind, w).start()

    def sum_second(h):
        for w in range(2):
            ring(h, 1, w).wait_recv()
            ring(h, 0, w).wait_recv()
            value = partial[h, rows_of(chip(2 * steps[w])), :] + ring_recv[h, 1, w].astype(F32)
            more = ring_recv[h, 0, w, :, part_of(w)].astype(F32)
            same = slice(w * quarter, (w + 1) * quarter)
            other = slice((1 - w) * quarter, (2 - w) * quarter)
            ring_send[h, 3, w, :, part_of(w)] = (value[:, same] + more).astype(BF16)
            ring_send[h, 3, w, :, part_of(1 - w)] = value[:, other].astype(BF16)
            ring(h, 3, w).start()

    def sum_end(h):
        value = partial[h, rows_of(z), :]
        for kind in (2, 3):
            for w in range(2):
                ring(h, kind, w).wait_recv()
                value += ring_recv[h, kind, w].astype(F32)
        total[h, rows_of(z), :] = value.astype(BF16)

    def spread(h, kind, w):
        begun = chip((0, 0, -2, -2)[kind] * steps[w])
        piece = total.at[h, rows_of(begun)]
        if kind == 3:
            piece = piece.at[:, part_of(w)]
        return remote(
            piece,
            piece,
            sems.at[14 + h],
            spread_sems.at[h, kind, w],
            "dp",
            2 * chip(steps[w] * (2, 1, 1, 2)[kind]) + core,
        )

    def across(h, distance, side):
        half_rows = (core + side - 2 * core * side) * hrows
        piece = total.at[
            h, pl.ds(pl.multiple_of(half_rows + chip(distance) * prow, prow), prow)
        ]
        return remote(
            piece, piece, sems.at[16 + h], across_sems.at[h, distance + 3], "dp", partner
        )

    def cross(h, distance):
        across(h, distance, 0).start()

    def spread_first(h):
        for kind in (0, 1):
            for w in range(2):
                spread(h, kind, w).start()
        cross(h, 0)

    def spread_second(h):
        for w in range(2):
            spread(h, 0, w).wait_recv()
            spread(h, 2, w).start()
            spread(h, 3, w).start()
            cross(h, -2 * steps[w])

    def spread_near(h):
        for w in range(2):
            spread(h, 1, w).wait_recv()
            cross(h, -steps[w])

    def spread_far(h):
        for w in range(2):
            spread(h, 2, w).wait_recv()
            cross(h, -3 * steps[w])
        for w in range(2):
            spread(h, 3, w).wait_recv()
        cross(h, 4)

    def update(distance, side):
        if side == 1:
            for h in range(2):
                across(h, distance, 1).wait_recv()
        half_rows = (core + side - 2 * core * side) * hrows
        block = pl.ds(pl.multiple_of(half_rows + chip(distance) * prow, prow), prow)
        values = [total[h, block, :].astype(F32) for h in range(2)]
        square = values[0] * values[0] + values[1] * values[1]
        new = state_col[block, :] + jnp.sum(square, axis=1, keepdims=True) / width
        state_col[block, :] = new
        rate = LEARN_RATE / jnp.sqrt(new)
        for h in range(2):
            for part in range(2):
                columns = pl.ds(part * half + h * quarter, quarter)
                value = values[h][:, part * quarter : (part + 1) * quarter]
                out_table[block, columns] = table[block, columns] - value * rate

    own_part(0)
    own_part(1)
    all_rows(gr_send.at[0], gr_recv.at[0], 4).wait_send()
    start_rows(gr_send.at[1], gr_recv.at[1], 6)
    collect(0)
    take_pair(0)
    sum_first(0)
    sum_second(0)
    collect(1)
    sum_end(0)
    spread_first(0)
    take_pair(1)
    sum_first(1)
    spread_second(0)
    sum_second(1)
    spread_near(0)
    sum_end(1)
    spread_first(1)
    spread_far(0)
    spread_second(1)
    spread_near(1)
    for side in range(2):
        for distance in (0, 2, -2, 1, -1):
            update(distance, side)
    spread_far(1)
    for side in range(2):
        for distance in (3, -3, 4):
            update(distance, side)
    out_state[...] = to_row(state_col[...])
    all_rows(gr_send.at[1], gr_recv.at[1], 6).wait_send()
    for h in range(2):
        pair(h).wait_send()
        pieces = total.at[h, pl.ds(0, (nz - 1) * prow)]
        remote(pieces, pieces, sems.at[12 + h], sems.at[12 + h], "dp", partner).wait_send()
        remote(pieces, pieces, sems.at[14 + h], sems.at[14 + h], "dp", partner).wait_send()
        pieces = total.at[h, ours]
        remote(pieces, pieces, sems.at[16 + h], sems.at[16 + h], "dp", partner).wait_send()


def on_device(
    n_ent,
    n_dp,
    entity_table,
    adagrad_state,
    relation_phase,
    head_owner,
    head_row,
    relation_id,
    tail_row,
    negative_row,
):
    rows, width = entity_table.shape
    rels, half = relation_phase.shape
    tri = head_row.shape[0]
    negs = negative_row.shape[0]
    cap = 12
    slots = n_ent * cap
    chunks = width // LANES
    hrows = rows // 2
    prow = rows // n_dp
    nz = n_dp // 2
    vmem = pl.BlockSpec(memory_space=pltpu.VMEM)
    hbm = pl.BlockSpec(memory_space=pltpu.HBM)
    new_table, new_state = pl.pallas_call(
        functools.partial(kernel, n_ent, n_dp, cap),
        out_shape=(
            jax.ShapeDtypeStruct((rows, width), F32),
            jax.ShapeDtypeStruct((1, rows), F32),
        ),
        in_specs=[hbm] * 8,
        out_specs=(vmem, vmem),
        scratch_shapes=[
            pltpu.VMEM((rows, width), F32),
            pltpu.VMEM((rows, width), BF16),
            pltpu.VMEM((rels, half), F32),
            pltpu.VMEM((1, rows), F32),
            pltpu.VMEM((1, tri), jnp.int32),
            pltpu.VMEM((1, tri), jnp.int32),
            pltpu.VMEM((1, tri), jnp.int32),
            pltpu.VMEM((1, tri), jnp.int32),
            pltpu.VMEM((1, negs), jnp.int32),
            pltpu.VMEM((n_ent, 1, LANES), F32),
            pltpu.VMEM((n_ent, 1, LANES), F32),
            pltpu.VMEM((2, slots * chunks // 2, LANES), BF16),
            pltpu.VMEM((2, slots * chunks // 2, LANES), BF16),
            pltpu.VMEM((2, slots * chunks // 2, LANES), BF16),
            pltpu.VMEM((2, slots * chunks // 2, LANES), BF16),
            pltpu.VMEM((tri, slots), BF16),
            pltpu.VMEM((slots, tri), BF16),
            pltpu.VMEM((rows, slots), BF16),
            pltpu.VMEM((slots, rows), BF16),
            pltpu.VMEM((rows, tri), BF16),
            pltpu.VMEM((1, rows), F32),
            pltpu.VMEM((1, rows), F32),
            pltpu.VMEM((tri, width), F32),
            pltpu.VMEM((tri, half), F32),
            pltpu.VMEM((tri, half), F32),
            pltpu.VMEM((tri, width), F32),
            pltpu.VMEM((2, rows, half), F32),
            pltpu.VMEM((2, hrows, half), BF16),
            pltpu.VMEM((2, hrows, half), BF16),
            pltpu.VMEM((2, 4, 2, prow, half), BF16),
            pltpu.VMEM((2, 4, 2, prow, half), BF16),
            pltpu.VMEM((2, rows, half), BF16),
            pltpu.VMEM((rows, 1), F32),
            pltpu.VMEM((slots * chunks // 2, LANES), F32),
            pltpu.VMEM((slots * chunks // 2, LANES), F32),
            pltpu.SemaphoreType.DMA((20,)),
            pltpu.SemaphoreType.DMA((8,)),
            pltpu.SemaphoreType.DMA((2, 4, 2)),
            pltpu.SemaphoreType.DMA((2, 4, 2)),
            pltpu.SemaphoreType.DMA((2, 8)),
        ],
        compiler_params=pltpu.CompilerParams(
            collective_id=0, has_side_effects=True, vmem_limit_bytes=48 * 1024 * 1024
        ),
    )(*[pltpu.with_memory_space_constraint(a, pltpu.HBM) for a in (
        entity_table,
        adagrad_state.reshape(1, rows),
        relation_phase,
        head_owner.reshape(1, tri),
        head_row.reshape(1, tri),
        relation_id.reshape(1, tri),
        tail_row.reshape(1, tri),
        negative_row.reshape(1, negs),
    )])
    return new_table, new_state.reshape(rows)


def solution(mesh):
    return jax.shard_map(
        functools.partial(on_device, mesh.shape["ent"], mesh.shape["dp"]),
        mesh=mesh,
        in_specs=(
            P("ent", None),
            P("ent"),
            P(),
            P(("dp", "ent"), None),
            P(("dp", "ent")),
            P(("dp", "ent")),
            P(("dp", "ent")),
            P(("dp", "ent")),
        ),
        out_specs=(P("ent", None), P("ent")),
        check_vma=False,
    )
```
